512 devices in a mesh: dp: 16 (over z_hi, x, core), expert: 32 (over y, z_lo).
Axes of the slice: x: 4, y: 4, z: 16 (z_hi: 2, z_lo: 8; z = z_hi * 8 + z_lo), core: 2. Of those that a mesh axis runs over, the one named last changes fastest.
Arguments:
- tokens: bfloat16 [65536, 512], P(('dp', 'expert')), may hold values from -6 to 6
- slot_order: int32 [512, 128], P(('dp', 'expert')), may hold values from 0 to 127, each once within a row
- centroid: bfloat16 [32, 512], P('expert'), may hold values from -0.25 to 0.25
- weight_in: bfloat16 [32, 512, 4096], P('expert', None, 'dp'), may hold values from -0.25 to 0.25
- weight_out: bfloat16 [32, 4096, 512], P('expert', 'dp'), may hold values from -0.09375 to 0.09375
- out_grad: bfloat16 [65536, 512], P(('dp', 'expert')), may hold values from -1.5 to 1.5
Outputs:
- layer_out: bfloat16 [65536, 512], P(('dp', 'expert'))
- grad_tokens: bfloat16 [65536, 512], P(('dp', 'expert'))
- grad_centroid: float32 [32, 512], P('expert')
- grad_in: float32 [32, 512, 4096], P('expert', None, 'dp')
- grad_out: float32 [32, 4096, 512], P('expert', 'dp')
The draws below stay inside these ranges and needn't reach their ends.
Inputs may be any that keep to these rules, and one draw needn't show every extreme that they name: `slot_order`: in each row (one device, rows in the order of the devices of dp+expert) every number below 128 appears once; entries 4 * e to 4 * e + 3 name the tokens of that device that go to expert e.
All inputs are finite; a program needn't handle non-finite values.
Results may differ from the reference program's by a relative error of at most 0.015.
Values may be sent and summed in bfloat16 or wider, within the bound.
No kernel may reach another device: no remote copies, remote signals or barrier semaphores. Data moves between devices by JAX's collectives and lax.ppermute only.
A program may use at most 64 MiB of HBM per device.

```python
import jax
import jax.numpy as jnp
from jax import lax

D = 512
FF = 4096
TOK_DEV = 128
EXPERTS = 32
BLK = 4
FF_DEV = 256
TOKENS = 65536
N_DP = 16
N_EXPERT = 32


def shard_levels(stream_key, extent, split, smallest, top_value):
    gain, own = 1.0, jax.random.fold_in(stream_key, 6)
    for position, parts in split:
        draws = jnp.exp(jax.random.uniform(jax.random.fold_in(own, position), (parts,), jnp.float32, smallest / len(split), top_value / len(split)))
        gain = gain * jnp.repeat(draws, extent[position] // parts).reshape([-1 if axis == position else 1 for axis in range(len(extent))])
    return gain


def bell_draw(stream_key, dims, width, reach, cuts=(), kind=jnp.bfloat16):
    array = width * jax.random.normal(stream_key, dims, jnp.float32)
    if cuts:
        array = array * shard_levels(stream_key, dims, cuts, -0.22, 0.18)
    return jnp.clip(array, -reach, reach).astype(kind)


def setup_inputs(seed: int = 0) -> dict:
    streams_of = jax.random.split(jax.random.key(seed), 7)
    return {
        "tokens": bell_draw(streams_of[0], (TOKENS, D), 1.0, 6.0, ((0, 512),)),
        "slot_order": jax.vmap(lambda own: jax.random.permutation(own, TOK_DEV))(jax.random.split(streams_of[1], (N_DP * N_EXPERT))).reshape((N_DP * N_EXPERT, TOK_DEV)).astype(jnp.int32),
        "centroid": bell_draw(streams_of[2], (EXPERTS, D), D ** -0.5, 0.25, ((0, 32),)),
        "weight_in": bell_draw(streams_of[3], (EXPERTS, D, FF), D ** -0.5, 0.25, ((0, 32), (2, 16))),
        "weight_out": bell_draw(streams_of[4], (EXPERTS, FF, D), FF ** -0.5, 0.09375, ((0, 32), (1, 16))),
        "out_grad": bell_draw(streams_of[5], (TOKENS, D), 0.25, 1.5, ((0, 512),)),
    }


def smooth(values):
    return jax.nn.gelu(values, approximate=True)

def rounded_sum(partials):
    narrow = lax.optimization_barrier(partials.astype(jnp.bfloat16))
    return lax.optimization_barrier(jnp.sum(narrow.astype(jnp.float32), axis=0))

def one_expert(tokens, out_grad, row_index, centroid_row, first_weight, second_weight):
    routed = tokens[row_index]
    d_routed = out_grad[row_index]
    row_count = row_index.shape[0]
    gating = jax.nn.sigmoid(jnp.dot(routed, centroid_row, preferred_element_type=jnp.float32))
    pre_act = jnp.dot(routed, first_weight, preferred_element_type=jnp.float32)
    hidden = smooth(pre_act).astype(jnp.bfloat16)
    partials = jnp.einsum('rqf,qfd->qrd', hidden.astype(jnp.float32).reshape(row_count, N_DP, FF_DEV), second_weight.astype(jnp.float32).reshape(N_DP, FF_DEV, D))
    expert_out = rounded_sum(partials)
    layer_rows = (routed.astype(jnp.float32) + gating[:, None] * expert_out).astype(jnp.bfloat16)
    d_expert = (gating[:, None] * d_routed.astype(jnp.float32)).astype(jnp.bfloat16)
    d_logit = lax.optimization_barrier(jnp.sum(d_routed.astype(jnp.float32) * expert_out, axis=1)) * gating * (1.0 - gating)
    centroid_grad = jnp.dot(d_logit, routed.astype(jnp.float32), precision=lax.Precision.HIGHEST)
    second_grad = jnp.dot(hidden.T, d_expert, preferred_element_type=jnp.float32)
    back_grad = jnp.dot(d_expert, second_weight.T, preferred_element_type=jnp.float32)
    d_hidden = jax.vjp(smooth, pre_act)[1](back_grad)[0].astype(jnp.bfloat16)
    first_grad = jnp.dot(routed.T, d_hidden, preferred_element_type=jnp.float32)
    inner_parts = jnp.einsum('rqf,dqf->qrd', d_hidden.astype(jnp.float32).reshape(row_count, N_DP, FF_DEV), first_weight.astype(jnp.float32).reshape(D, N_DP, FF_DEV))
    inner_grad = rounded_sum(inner_parts)
    grad_rows = (d_routed.astype(jnp.float32) + d_logit[:, None] * centroid_row.astype(jnp.float32) + inner_grad).astype(jnp.bfloat16)
    return (layer_rows, grad_rows, centroid_grad, first_grad, second_grad)

def reference(tokens, slot_order, centroid, weight_in, weight_out, out_grad):
    devices = slot_order.shape[0]
    row_base = (jnp.arange(devices, dtype=jnp.int32) * TOK_DEV)[:, None]
    expert_rows = (row_base + slot_order.astype(jnp.int32)).astype(jnp.int32).reshape(devices, EXPERTS, BLK)
    expert_rows = jnp.transpose(expert_rows, (1, 0, 2)).reshape(EXPERTS, devices * BLK)

    def per_expert(inputs):
        row_index, centroid_row, first_weight, second_weight = inputs
        return one_expert(tokens, out_grad, row_index, centroid_row, first_weight, second_weight)
    layer_rows, grad_rows, grad_centroid, grad_in, grad_out = lax.map(per_expert, (expert_rows, centroid, weight_in, weight_out))
    flat_rows = expert_rows.reshape(-1)
    layer_out = jnp.zeros_like(tokens).at[flat_rows].set(layer_rows.reshape(-1, D))
    grad_tokens = jnp.zeros_like(tokens).at[flat_rows].set(grad_rows.reshape(-1, D))
    return (layer_out, grad_tokens, grad_centroid, grad_in, grad_out)
```

```python
import math

import jax
import jax.numpy as jnp
from jax import lax
from jax.experimental import pallas as pl
from jax.experimental.pallas import tpu as pltpu
from jax.sharding import Mesh
from jax.sharding import PartitionSpec as P

BF = jnp.bfloat16
F32 = jnp.float32
ZH, X, CORE, Y, ZL = 2, 4, 2, 4, 8
EXPERTS = Y * ZL
BLK = 4
D = 512
TOK = EXPERTS * BLK
ROWS = ZH * TOK
MIXED = 2 * ROWS
UNITS = 256
HALF = D // 2
PACKED = D + 2 * UNITS
NOTE = 16
VMEM_LIMIT = 16 * 1024 * 1024


def dot(a, b, ca=1, cb=0):
    return lax.dot_general(a, b, (((ca,), (cb,)), ((), ())), preferred_element_type=F32)


def iota(shape, axis):
    return lax.broadcasted_iota(jnp.int32, shape, axis)


def mixed_picks(rows, on_rows_first):
    shape = (rows, 2 * rows) if on_rows_first else (2 * rows, rows)
    plain = iota(shape, 0 if on_rows_first else 1)
    mixed = iota(shape, 1 if on_rows_first else 0)
    place = (plain // BLK) * (2 * BLK) + plain % BLK
    return (mixed == place).astype(BF), (mixed == place + BLK).astype(BF)


def pack_kernel(order_ref, tok_ref, grad_ref, out_ref):
    token_pick, grad_pick = mixed_picks(TOK, True)
    order = jnp.broadcast_to(order_ref[...].astype(F32), (8, TOK)).astype(BF)
    source = iota((TOK, 2 * TOK), 0).astype(F32)
    token_source = dot(order, token_pick)[0:1]
    grad_source = dot(order, grad_pick)[0:1]
    kind = (iota((TOK, 2 * TOK), 1) // BLK) % 2
    pick_token = ((source == token_source) & (kind == 0)).astype(BF)
    pick_grad = ((source == grad_source) & (kind == 1)).astype(BF)
    mixed = (dot(pick_token, tok_ref[...], 0, 0) + dot(pick_grad, grad_ref[...], 0, 0)).astype(BF)
    for half in range(ZH):
        out_ref[half * 2 * TOK : (half + 1) * 2 * TOK, :] = mixed


def expert_kernel(
    rows_ref, centroid_ref, s0, s1, s2, s3,
    mixed_ref, centroid_grad_ref, routed_ref, d_expert_ref, hidden_ref, d_hidden_ref,
):
    token_pick, grad_pick = mixed_picks(ROWS, True)
    received = rows_ref[...]
    routed = dot(token_pick, received)
    d_routed = dot(grad_pick, received)
    centroid = centroid_ref[...].astype(F32)
    gating = jax.nn.sigmoid(jnp.sum(routed * centroid, axis=1, keepdims=True))
    routed_half = routed.astype(BF)
    d_expert = (gating * d_routed).astype(BF)
    routed_ref[...] = routed_half
    d_expert_ref[...] = d_expert
    out_part = jnp.zeros((ROWS, D), F32)
    inner_part = jnp.zeros((ROWS, D), F32)
    scale = math.sqrt(2.0 / math.pi)
    d_expert_a, d_expert_b = d_expert[:, :HALF], d_expert[:, HALF:]
    for k, shard in enumerate((s0, s1, s2, s3)):
        w = shard[:D, :]
        v_a, v_b = shard[D : D + UNITS, :], shard[D + UNITS :, :]
        pre = dot(routed_half, w)
        square = pre * pre
        bend = jnp.tanh(scale * pre * (1.0 + 0.044715 * square))
        half_up = 0.5 * (1.0 + bend)
        hidden = (pre * half_up).astype(BF)
        slope = half_up + 0.5 * pre * (1.0 - bend * bend) * (
            scale * (1.0 + 3.0 * 0.044715 * square)
        )
        back = dot(d_expert_a, v_a, 1, 1) + dot(d_expert_b, v_b, 1, 1)
        d_hidden = (back * slope).astype(BF)
        out_part += jnp.concatenate([dot(hidden, v_a), dot(hidden, v_b)], axis=1)
        inner_part += dot(d_hidden, w, 1, 1)
        hidden_ref[:, k * UNITS : (k + 1) * UNITS] = hidden
        d_hidden_ref[:, k * UNITS : (k + 1) * UNITS] = d_hidden
    d_logit = jnp.sum(d_routed * out_part, axis=1, keepdims=True) * gating * (1.0 - gating)
    centroid_grad_ref[...] = jnp.sum(d_logit * routed, axis=0, keepdims=True)
    layer_part = (gating * out_part).astype(BF)
    grad_part = (inner_part + d_logit * centroid).astype(BF)
    token_place, grad_place = mixed_picks(ROWS, False)
    mixed_ref[...] = (dot(token_place, layer_part) + dot(grad_place, grad_part)).astype(BF)


def weight_grad_kernel(
    centroid_a, routed_a, d_expert_a, hidden_a, d_hidden_a,
    centroid_b, routed_b, d_expert_b, hidden_b, d_hidden_b,
    own_in, own_out, own_centroid, *sent,
):
    centroid_grad = centroid_a[...] + centroid_b[...]
    own_centroid[...] = centroid_grad
    high = centroid_grad.astype(BF).astype(F32)
    row = iota((NOTE, D), 0)
    note = jnp.where(row == 0, high, jnp.where(row == 1, centroid_grad - high, 0.0)).astype(BF)
    for k in range(X):
        units = slice(k * UNITS, (k + 1) * UNITS)
        first = dot(routed_a[...], d_hidden_a[:, units], 0, 0) + dot(
            routed_b[...], d_hidden_b[:, units], 0, 0
        )
        second = dot(hidden_a[:, units], d_expert_a[...], 0, 0) + dot(
            hidden_b[:, units], d_expert_b[...], 0, 0
        )
        if k == 0:
            own_in[...] = first
            own_out[...] = second
        else:
            packed = sent[k - 1]
            packed[:D, :] = first.astype(BF)
            packed[D : D + UNITS, :] = second[:, :HALF].astype(BF)
            packed[D + UNITS : PACKED, :] = second[:, HALF:].astype(BF)
            packed[PACKED : PACKED + NOTE, :] = note[:, :HALF]
            packed[PACKED + NOTE :, :] = note[:, HALF:]


def unpack_kernel(order_ref, home_ref, tok_ref, grad_ref, layer_ref, grad_out_ref):
    order = jnp.broadcast_to(order_ref[...].astype(F32), (8, TOK)).astype(BF)
    token = iota((TOK, 2 * TOK), 0).astype(F32)
    token_pick, grad_pick = mixed_picks(TOK, True)
    kind = (iota((TOK, 2 * TOK), 1) // BLK) % 2
    pick_token = ((token == dot(order, token_pick)[0:1]) & (kind == 0)).astype(BF)
    pick_grad = ((token == dot(order, grad_pick)[0:1]) & (kind == 1)).astype(BF)
    layer = tok_ref[...].astype(F32)
    grad = grad_ref[...].astype(F32)
    for half in range(ZH):
        rows = home_ref[half * 2 * TOK : (half + 1) * 2 * TOK, :]
        layer += dot(pick_token, rows)
        grad += dot(pick_grad, rows)
    layer_ref[...] = layer.astype(BF)
    grad_out_ref[...] = grad.astype(BF)


def call(kernel, shapes, *operands):
    return pl.pallas_call(
        kernel,
        out_shape=[jax.ShapeDtypeStruct(shape, dtype) for shape, dtype in shapes],
        compiler_params=pltpu.CompilerParams(vmem_limit_bytes=VMEM_LIMIT),
    )(*operands)


def shift(value, axis, size, by):
    return lax.ppermute(value, axis, [(i, (i + by) % size) for i in range(size)])


def on_device(tokens, slot_order, centroid, weight_in, weight_out, out_grad):
    second = weight_out[0]
    shard = jnp.concatenate([weight_in[0], second[:, :HALF], second[:, HALF:]], axis=0)
    shards = [shard] + [shift(shard, "x", X, -k) for k in range(1, X)]
    (packed,) = call(pack_kernel, [((MIXED, D), BF)], slot_order, tokens, out_grad)
    own_rows = lax.all_to_all(
        packed.reshape(ZH * EXPERTS, 2 * BLK, D), ("zh", "y", "zl"), 0, 0, tiled=True
    ).reshape(MIXED, D)
    other_rows = shift(own_rows, "core", CORE, 1)
    part_shapes = [
        ((MIXED, D), BF), ((1, D), F32), ((ROWS, D), BF), ((ROWS, D), BF),
        ((ROWS, X * UNITS), BF), ((ROWS, X * UNITS), BF),
    ]
    own = call(expert_kernel, part_shapes, own_rows, centroid, *shards)
    other = call(expert_kernel, part_shapes, other_rows, centroid, *shards)
    from_other = shift(other[0], "core", CORE, 1)
    grads = call(
        weight_grad_kernel,
        [((D, UNITS), F32), ((UNITS, D), F32), ((1, D), F32)]
        + [((PACKED + 2 * NOTE, UNITS), BF)] * (X - 1),
        *own[1:], *other[1:],
    )
    first_grad, second_grad, centroid_grad = grads[:3]
    for k in range(1, X):
        arrived = shift(grads[2 + k], "x", X, k).astype(F32)
        first_grad += arrived[:D]
        second_grad += jnp.concatenate([arrived[D : D + UNITS], arrived[D + UNITS : PACKED]], axis=1)
        note = jnp.concatenate([arrived[PACKED : PACKED + 2], arrived[PACKED + NOTE : PACKED + NOTE + 2]], axis=1)
        centroid_grad += note[0:1] + note[1:2]
    turns = [(1, 0), (0, 1), (1, 1)]
    grad_centroid = centroid_grad + sum(
        lax.ppermute(
            centroid_grad,
            ("zh", "core"),
            [(2 * a + b, 2 * (a ^ i) + (b ^ j)) for a in range(ZH) for b in range(CORE)],
        )
        for i, j in turns
    )
    returned = (own[0].astype(F32) + from_other.astype(F32)).astype(BF)
    home = lax.all_to_all(
        returned.reshape(ZH * EXPERTS, 2 * BLK, D), ("zh", "y", "zl"), 0, 0, tiled=True
    ).reshape(MIXED, D)
    layer_out, grad_tokens = call(
        unpack_kernel, [((TOK, D), BF), ((TOK, D), BF)], slot_order, home, tokens, out_grad
    )
    return (layer_out, grad_tokens, grad_centroid, first_grad[None], second_grad[None])


def solution(mesh):
    fine = Mesh(mesh.devices.reshape(ZH, X, CORE, Y, ZL), ("zh", "x", "core", "y", "zl"))
    dp, expert = ("zh", "x", "core"), ("y", "zl")
    both = dp + expert
    placed = (
        P(both, None),
        P(both, None),
        P(expert, None),
        P(expert, None, dp),
        P(expert, dp, None),
        P(both, None),
    )
    return jax.shard_map(
        on_device,
        mesh=fine,
        in_specs=placed,
        out_specs=(
            P(both, None),
            P(both, None),
            P(expert, None),
            P(expert, None, dp),
            P(expert, dp, None),
        ),
        check_vma=False,
    )
```

```python
import math

import jax
import jax.numpy as jnp
from jax import lax
from jax.experimental import pallas as pl
from jax.experimental.pallas import tpu as pltpu
from jax.sharding import Mesh
from jax.sharding import PartitionSpec as P

BF = jnp.bfloat16
F32 = jnp.float32
ZH, X, CORE, Y, ZL = 2, 4, 2, 4, 8
EXPERTS = Y * ZL
BLK = 4
D = 512
TOK = EXPERTS * BLK
ROWS = ZH * TOK
MIXED = 2 * ROWS
UNITS = 256
HALF = D // 2
PACKED = D + 2 * UNITS
SHARDS = X * CORE
VMEM_LIMIT = 16 * 1024 * 1024


def dot(a, b, ca=1, cb=0):
    return lax.dot_general(a, b, (((ca,), (cb,)), ((), ())), preferred_element_type=F32)


def iota(shape, axis):
    return lax.broadcasted_iota(jnp.int32, shape, axis)


def mixed_picks(rows, on_rows_first):
    shape = (rows, 2 * rows) if on_rows_first else (2 * rows, rows)
    plain = iota(shape, 0 if on_rows_first else 1)
    mixed = iota(shape, 1 if on_rows_first else 0)
    place = (plain // BLK) * (2 * BLK) + plain % BLK
    return (mixed == place).astype(BF), (mixed == place + BLK).astype(BF)


def pack_kernel(
    order_ref, tok_ref, grad_ref, first_ref, second_ref,
    out_ref, shard_ref, order_vmem, tok_vmem, grad_vmem, sems,
):
    copies = [
        pltpu.make_async_copy(source, target, sems.at[i])
        for i, (source, target) in enumerate(
            (
                (order_ref, order_vmem),
                (tok_ref, tok_vmem),
                (grad_ref, grad_vmem),
                (first_ref.at[0], shard_ref.at[:D, :]),
                (second_ref.at[0, :, :HALF], shard_ref.at[D : D + UNITS, :]),
                (second_ref.at[0, :, HALF:], shard_ref.at[D + UNITS :, :]),
            )
        )
    ]
    for copy in copies:
        copy.start()
    token_pick, grad_pick = mixed_picks(TOK, True)
    copies[0].wait()
    order = jnp.broadcast_to(order_vmem[...].astype(F32), (8, TOK)).astype(BF)
    source = iota((TOK, 2 * TOK), 0).astype(F32)
    token_source = dot(order, token_pick)[0:1]
    grad_source = dot(order, grad_pick)[0:1]
    kind = (iota((TOK, 2 * TOK), 1) // BLK) % 2
    pick_token = ((source == token_source) & (kind == 0)).astype(BF)
    pick_grad = ((source == grad_source) & (kind == 1)).astype(BF)
    copies[1].wait()
    mixed = dot(pick_token, tok_vmem[...], 0, 0)
    copies[2].wait()
    mixed = (mixed + dot(pick_grad, grad_vmem[...], 0, 0)).astype(BF)
    for half in range(ZH):
        out_ref[half * 2 * TOK : (half + 1) * 2 * TOK, :] = mixed
    for copy in copies[3:]:
        copy.wait()


def expert_kernel(
    rows_ref, centroid_ref, shards_ref,
    mixed_ref, centroid_grad_ref, routed_ref, d_expert_ref, hidden_ref, d_hidden_ref,
    shards_vmem, sems,
):
    copies = [
        pltpu.make_async_copy(
            shards_ref.at[k * PACKED : (k + 1) * PACKED, :], shards_vmem.at[k], sems.at[k]
        )
        for k in range(SHARDS)
    ]
    for copy in copies:
        copy.start()
    token_pick, grad_pick = mixed_picks(ROWS, True)
    received = rows_ref[...]
    routed = dot(token_pick, received)
    d_routed = dot(grad_pick, received)
    centroid = centroid_ref[...].astype(F32)
    gating = jax.nn.sigmoid(jnp.sum(routed * centroid, axis=1, keepdims=True))
    routed_half = routed.astype(BF)
    d_expert = (gating * d_routed).astype(BF)
    routed_ref[...] = routed_half
    d_expert_ref[...] = d_expert
    d_expert_a, d_expert_b = d_expert[:, :HALF], d_expert[:, HALF:]
    out_part = jnp.zeros((ROWS, D), F32)
    inner_part = jnp.zeros((ROWS, D), F32)
    scale = math.sqrt(2.0 / math.pi)
    for k in range(SHARDS):
        copies[k].wait()
        w = shards_vmem[k, :D, :]
        v_a, v_b = shards_vmem[k, D : D + UNITS, :], shards_vmem[k, D + UNITS :, :]
        pre = dot(routed_half, w)
        square = pre * pre
        bend = jnp.tanh(scale * pre * (1.0 + 0.044715 * square))
        half_up = 0.5 * (1.0 + bend)
        hidden = (pre * half_up).astype(BF)
        slope = half_up + 0.5 * pre * (1.0 - bend * bend) * (
            scale * (1.0 + 3.0 * 0.044715 * square)
        )
        back = dot(d_expert_a, v_a, 1, 1) + dot(d_expert_b, v_b, 1, 1)
        d_hidden = (back * slope).astype(BF)
        out_part += jnp.concatenate([dot(hidden, v_a), dot(hidden, v_b)], axis=1)
        inner_part += dot(d_hidden, w, 1, 1)
        hidden_ref[:, k * UNITS : (k + 1) * UNITS] = hidden
        d_hidden_ref[:, k * UNITS : (k + 1) * UNITS] = d_hidden
    d_logit = jnp.sum(d_routed * out_part, axis=1, keepdims=True) * gating * (1.0 - gating)
    centroid_grad_ref[...] = jnp.sum(d_logit * routed, axis=0, keepdims=True)
    layer_part = (gating * out_part).astype(BF)
    grad_part = (inner_part + d_logit * centroid).astype(BF)
    token_place, grad_place = mixed_picks(ROWS, False)
    mixed_ref[...] = (dot(token_place, layer_part) + dot(grad_place, grad_part)).astype(BF)


def weight_grad_kernel(
    routed_ref, d_expert_ref, hidden_ref, d_hidden_ref, packed_ref, packed_vmem, sems
):
    copies = []
    for k in range(SHARDS):
        units = slice(k * UNITS, (k + 1) * UNITS)
        first = dot(routed_ref[...], d_hidden_ref[:, units], 0, 0)
        second = dot(hidden_ref[:, units], d_expert_ref[...], 0, 0)
        packed_vmem[k, :D, :] = first.astype(BF)
        packed_vmem[k, D : D + UNITS, :] = second[:, :HALF].astype(BF)
        packed_vmem[k, D + UNITS :, :] = second[:, HALF:].astype(BF)
        copies.append(
            pltpu.make_async_copy(
                packed_vmem.at[k], packed_ref.at[k * PACKED : (k + 1) * PACKED, :], sems.at[k]
            )
        )
        copies[k].start()
    for copy in copies:
        copy.wait()


def spread_kernel(packed_ref, first_ref, second_ref):
    first_ref[0] = packed_ref[:D, :].astype(F32)
    second_ref[0, :, :HALF] = packed_ref[D : D + UNITS, :].astype(F32)
    second_ref[0, :, HALF:] = packed_ref[D + UNITS :, :].astype(F32)


def unpack_kernel(order_ref, home_ref, tok_ref, grad_ref, layer_ref, grad_out_ref):
    order = jnp.broadcast_to(order_ref[...].astype(F32), (8, TOK)).astype(BF)
    token = iota((TOK, 2 * TOK), 0).astype(F32)
    token_pick, grad_pick = mixed_picks(TOK, True)
    kind = (iota((TOK, 2 * TOK), 1) // BLK) % 2
    pick_token = ((token == dot(order, token_pick)[0:1]) & (kind == 0)).astype(BF)
    pick_grad = ((token == dot(order, grad_pick)[0:1]) & (kind == 1)).astype(BF)
    layer = tok_ref[...].astype(F32)
    grad = grad_ref[...].astype(F32)
    for half in range(ZH):
        rows = home_ref[half * 2 * TOK : (half + 1) * 2 * TOK, :]
        layer += dot(pick_token, rows)
        grad += dot(pick_grad, rows)
    layer_ref[...] = layer.astype(BF)
    grad_out_ref[...] = grad.astype(BF)


def in_hbm(value):
    return pltpu.with_memory_space_constraint(value, pltpu.HBM)


def hbm_out(shape, dtype):
    return pltpu.HBM(shape, dtype)


def call(kernel, outs, *operands, **options):
    return pl.pallas_call(
        kernel,
        out_shape=[
            out if hasattr(out, "memory_space") else jax.ShapeDtypeStruct(*out) for out in outs
        ],
        compiler_params=pltpu.CompilerParams(vmem_limit_bytes=VMEM_LIMIT),
        **options,
    )(*operands)


def on_device(tokens, slot_order, centroid, weight_in, weight_out, out_grad):
    vmem, hbm = pl.BlockSpec(memory_space=pltpu.VMEM), pl.BlockSpec(memory_space=pltpu.HBM)
    packed, shard = call(
        pack_kernel,
        [((MIXED, D), BF), hbm_out((PACKED, UNITS), BF)],
        *(in_hbm(each) for each in (slot_order, tokens, out_grad, weight_in, weight_out)),
        in_specs=[hbm] * 5,
        out_specs=[vmem, hbm],
        scratch_shapes=[
            pltpu.VMEM((1, TOK), jnp.int32),
            pltpu.VMEM((TOK, D), BF),
            pltpu.VMEM((TOK, D), BF),
            pltpu.SemaphoreType.DMA((6,)),
        ],
    )
    shards = lax.all_gather(shard, ("x", "core"), axis=0, tiled=True)
    rows = lax.all_to_all(
        packed.reshape(ZH * EXPERTS, 2 * BLK, D), ("zh", "y", "zl"), 0, 0, tiled=True
    ).reshape(MIXED, D)
    mixed, centroid_term, *kept = call(
        expert_kernel,
        [
            ((MIXED, D), BF), ((1, D), F32), ((ROWS, D), BF), ((ROWS, D), BF),
            ((ROWS, SHARDS * UNITS), BF), ((ROWS, SHARDS * UNITS), BF),
        ],
        rows, centroid, in_hbm(shards),
        in_specs=[vmem, vmem, hbm],
        out_specs=[vmem] * 6,
        scratch_shapes=[
            pltpu.VMEM((SHARDS, PACKED, UNITS), BF), pltpu.SemaphoreType.DMA((SHARDS,)),
        ],
    )
    home = lax.all_to_all(
        mixed.reshape(ZH * EXPERTS, 2 * BLK, D), ("zh", "y", "zl"), 0, 0, tiled=True
    ).reshape(MIXED, D)
    (packed_grads,) = call(
        weight_grad_kernel,
        [hbm_out((SHARDS * PACKED, UNITS), BF)],
        *kept,
        in_specs=[vmem] * 4,
        out_specs=[hbm],
        scratch_shapes=[
            pltpu.VMEM((SHARDS, PACKED, UNITS), BF), pltpu.SemaphoreType.DMA((SHARDS,)),
        ],
    )
    grads = lax.psum_scatter(packed_grads, ("x", "core"), scatter_dimension=0, tiled=True)
    first_grad, second_grad = call(
        spread_kernel, [((1, D, UNITS), F32), ((1, UNITS, D), F32)], grads
    )
    centroid_terms = lax.all_gather(centroid_term, ("zh", "x", "core"), axis=0, tiled=True)
    grad_centroid = jnp.sum(centroid_terms, axis=0, keepdims=True)
    layer_out, grad_tokens = call(
        unpack_kernel, [((TOK, D), BF), ((TOK, D), BF)], slot_order, home, tokens, out_grad
    )
    return (layer_out, grad_tokens, grad_centroid, first_grad, second_grad)


def solution(mesh):
    fine = Mesh(mesh.devices.reshape(ZH, X, CORE, Y, ZL), ("zh", "x", "core", "y", "zl"))
    dp, expert = ("zh", "x", "core"), ("y", "zl")
    both = dp + expert
    placed = (
        P(both, None),
        P(both, None),
        P(expert, None),
        P(expert, None, dp),
        P(expert, dp, None),
        P(both, None),
    )
    return jax.shard_map(
        on_device,
        mesh=fine,
        in_specs=placed,
        out_specs=(
            P(both, None),
            P(both, None),
            P(expert, None),
            P(expert, None, dp),
            P(expert, dp, None),
        ),
        check_vma=False,
    )
```

```python
import math

import jax
import jax.numpy as jnp
from jax import lax
from jax.experimental import pallas as pl
from jax.experimental.pallas import tpu as pltpu
from jax.sharding import Mesh
from jax.sharding import PartitionSpec as P

BF = jnp.bfloat16
F32 = jnp.float32
ZH, X, CORE, Y, ZL = 2, 4, 2, 4, 8
EXPERTS = Y * ZL
BLK = 4
D = 512
TOK = EXPERTS * BLK
ROWS = ZH * TOK
MIXED = 2 * ROWS
UNITS = 256
HALF = D // 2
PACKED = D + 2 * UNITS
NOTE = 16
VMEM_LIMIT = 16 * 1024 * 1024


def dot(a, b, ca=1, cb=0):
    return lax.dot_general(a, b, (((ca,), (cb,)), ((), ())), preferred_element_type=F32)


def iota(shape, axis):
    return lax.broadcasted_iota(jnp.int32, shape, axis)


def mixed_picks(rows, on_rows_first):
    shape = (rows, 2 * rows) if on_rows_first else (2 * rows, rows)
    plain = iota(shape, 0 if on_rows_first else 1)
    mixed = iota(shape, 1 if on_rows_first else 0)
    place = (plain // BLK) * (2 * BLK) + plain % BLK
    return (mixed == place).astype(BF), (mixed == place + BLK).astype(BF)


def pack_kernel(
    order_ref, tok_ref, grad_ref, out_ref, order_vmem, tok_vmem, grad_vmem, sems
):
    copies = [
        pltpu.make_async_copy(source, target, sems.at[i])
        for i, (source, target) in enumerate(
            ((order_ref, order_vmem), (tok_ref, tok_vmem), (grad_ref, grad_vmem))
        )
    ]
    for copy in copies:
        copy.start()
    token_pick, grad_pick = mixed_picks(TOK, True)
    source = iota((TOK, 2 * TOK), 0).astype(F32)
    kind = (iota((TOK, 2 * TOK), 1) // BLK) % 2
    copies[0].wait()
    order = jnp.broadcast_to(order_vmem[...].astype(F32), (8, TOK)).astype(BF)
    token_source = dot(order, token_pick)[0:1]
    grad_source = dot(order, grad_pick)[0:1]
    pick_token = ((source == token_source) & (kind == 0)).astype(BF)
    pick_grad = ((source == grad_source) & (kind == 1)).astype(BF)
    copies[1].wait()
    mixed = dot(pick_token, tok_vmem[...], 0, 0)
    copies[2].wait()
    mixed = (mixed + dot(pick_grad, grad_vmem[...], 0, 0)).astype(BF)
    for half in range(ZH):
        out_ref[half * 2 * TOK : (half + 1) * 2 * TOK, :] = mixed


def expert_kernel(
    rows_ref, centroid_ref, before_ref, s0, s1, s2, s3,
    mixed_ref, centroid_grad_ref, routed_ref, d_expert_ref, hidden_ref, d_hidden_ref,
):
    token_pick, grad_pick = mixed_picks(ROWS, True)
    received = rows_ref[...]
    routed = dot(token_pick, received)
    d_routed = dot(grad_pick, received)
    centroid = centroid_ref[...].astype(F32)
    gating = jax.nn.sigmoid(jnp.sum(routed * centroid, axis=1, keepdims=True))
    routed_half = routed.astype(BF)
    d_expert = (gating * d_routed).astype(BF)
    routed_ref[...] = routed_half
    d_expert_ref[...] = d_expert
    out_part = jnp.zeros((ROWS, D), F32)
    inner_part = jnp.zeros((ROWS, D), F32)
    scale = math.sqrt(2.0 / math.pi)
    d_expert_a, d_expert_b = d_expert[:, :HALF], d_expert[:, HALF:]
    for k, shard in enumerate((s0, s1, s2, s3)):
        w = shard[:D, :]
        v_a, v_b = shard[D : D + UNITS, :], shard[D + UNITS :, :]
        pre = dot(routed_half, w)
        square = pre * pre
        bend = jnp.tanh(scale * pre * (1.0 + 0.044715 * square))
        half_up = 0.5 * (1.0 + bend)
        hidden = (pre * half_up).astype(BF)
        slope = half_up + 0.5 * pre * (1.0 - bend * bend) * (
            scale * (1.0 + 3.0 * 0.044715 * square)
        )
        back = dot(d_expert_a, v_a, 1, 1) + dot(d_expert_b, v_b, 1, 1)
        d_hidden = (back * slope).astype(BF)
        out_part += jnp.concatenate([dot(hidden, v_a), dot(hidden, v_b)], axis=1)
        inner_part += dot(d_hidden, w, 1, 1)
        hidden_ref[:, k * UNITS : (k + 1) * UNITS] = hidden
        d_hidden_ref[:, k * UNITS : (k + 1) * UNITS] = d_hidden
    d_logit = jnp.sum(d_routed * out_part, axis=1, keepdims=True) * gating * (1.0 - gating)
    centroid_grad = before_ref[...] + jnp.sum(d_logit * routed, axis=0, keepdims=True)
    centroid_grad_ref[...] = centroid_grad
    layer_part = (gating * out_part).astype(BF)
    grad_part = (inner_part + d_logit * centroid).astype(BF)
    token_place, grad_place = mixed_picks(ROWS, False)
    mixed_ref[:MIXED, :] = (dot(token_place, layer_part) + dot(grad_place, grad_part)).astype(BF)
    high = centroid_grad.astype(BF).astype(F32)
    row = iota((NOTE, D), 0)
    note = jnp.where(row == 0, high, jnp.where(row == 1, centroid_grad - high, 0.0))
    mixed_ref[MIXED:, :] = note.astype(BF)


def join_kernel(own_ref, other_ref, own_centroid_ref, out_ref, centroid_grad_ref):
    out_ref[...] = (own_ref[:MIXED, :].astype(F32) + other_ref[:MIXED, :].astype(F32)).astype(BF)
    note = other_ref[MIXED:, :].astype(F32)
    centroid_grad_ref[...] = own_centroid_ref[...] + note[0:1] + note[1:2]


def weight_grad_kernel(
    routed_a, d_expert_a, hidden_a, d_hidden_a, routed_b, d_expert_b, hidden_b, d_hidden_b,
    after_ref, own_in, own_out, *sent,
):
    for k in range(X):
        units = slice(k * UNITS, (k + 1) * UNITS)
        first = dot(routed_a[...], d_hidden_a[:, units], 0, 0) + dot(
            routed_b[...], d_hidden_b[:, units], 0, 0
        )
        second = dot(hidden_a[:, units], d_expert_a[...], 0, 0) + dot(
            hidden_b[:, units], d_expert_b[...], 0, 0
        )
        if k == 0:
            own_in[...] = first
            own_out[...] = second
        else:
            packed = sent[k - 1]
            packed[:D, :] = first.astype(BF)
            packed[D : D + UNITS, :] = second[:, :HALF].astype(BF)
            packed[D + UNITS :, :] = second[:, HALF:].astype(BF)


def total_kernel(own_in, own_out, p1, p2, p3, first_ref, second_ref):
    def total(rows):
        return p1[rows, :].astype(F32) + p2[rows, :].astype(F32) + p3[rows, :].astype(F32)

    first_ref[0] = own_in[...] + total(slice(0, D))
    second_ref[0, :, :HALF] = own_out[:, :HALF] + total(slice(D, D + UNITS))
    second_ref[0, :, HALF:] = own_out[:, HALF:] + total(slice(D + UNITS, PACKED))


def unpack_kernel(order_ref, home_ref, tok_ref, grad_ref, layer_ref, grad_out_ref):
    order = jnp.broadcast_to(order_ref[...].astype(F32), (8, TOK)).astype(BF)
    token = iota((TOK, 2 * TOK), 0).astype(F32)
    token_pick, grad_pick = mixed_picks(TOK, True)
    kind = (iota((TOK, 2 * TOK), 1) // BLK) % 2
    pick_token = ((token == dot(order, token_pick)[0:1]) & (kind == 0)).astype(BF)
    pick_grad = ((token == dot(order, grad_pick)[0:1]) & (kind == 1)).astype(BF)
    layer = tok_ref[...].astype(F32)
    grad = grad_ref[...].astype(F32)
    for half in range(ZH):
        rows = home_ref[half * 2 * TOK : (half + 1) * 2 * TOK, :]
        layer += dot(pick_token, rows)
        grad += dot(pick_grad, rows)
    layer_ref[...] = layer.astype(BF)
    grad_out_ref[...] = grad.astype(BF)


def in_hbm(value):
    return pltpu.with_memory_space_constraint(value, pltpu.HBM)


def call(kernel, outs, *operands, **options):
    return pl.pallas_call(
        kernel,
        out_shape=[jax.ShapeDtypeStruct(*out) for out in outs],
        compiler_params=pltpu.CompilerParams(vmem_limit_bytes=VMEM_LIMIT),
        **options,
    )(*operands)


def shift(value, axis, size, by):
    return lax.ppermute(value, axis, [(i, (i + by) % size) for i in range(size)])


def on_device(tokens, slot_order, centroid, weight_in, weight_out, out_grad):
    vmem, hbm = pl.BlockSpec(memory_space=pltpu.VMEM), pl.BlockSpec(memory_space=pltpu.HBM)
    second = weight_out[0]
    shard = jnp.concatenate([weight_in[0], second[:, :HALF], second[:, HALF:]], axis=0)
    shards = [shard] + [shift(shard, "x", X, -k) for k in range(1, X)]
    (packed,) = call(
        pack_kernel,
        [((MIXED, D), BF)],
        *(in_hbm(each) for each in (slot_order, tokens, out_grad)),
        in_specs=[hbm] * 3,
        out_specs=[vmem],
        scratch_shapes=[
            pltpu.VMEM((1, TOK), jnp.int32),
            pltpu.VMEM((TOK, D), BF),
            pltpu.VMEM((TOK, D), BF),
            pltpu.SemaphoreType.DMA((3,)),
        ],
    )
    own_rows = lax.all_to_all(
        packed.reshape(ZH * EXPERTS, 2 * BLK, D), ("zh", "y", "zl"), 0, 0, tiled=True
    ).reshape(MIXED, D)
    other_rows = shift(own_rows, "core", CORE, 1)
    part_shapes = [
        ((MIXED + NOTE, D), BF), ((1, D), F32), ((ROWS, D), BF), ((ROWS, D), BF),
        ((ROWS, X * UNITS), BF), ((ROWS, X * UNITS), BF),
    ]
    nothing = jnp.zeros((1, D), F32)
    own = call(expert_kernel, part_shapes, own_rows, centroid, nothing, *shards)
    other = call(expert_kernel, part_shapes, other_rows, centroid, own[1], *shards)
    from_other = shift(other[0], "core", CORE, 1)
    returned, centroid_grad = call(
        join_kernel, [((MIXED, D), BF), ((1, D), F32)], own[0], from_other, other[1]
    )
    home = lax.all_to_all(
        returned.reshape(ZH * EXPERTS, 2 * BLK, D), ("zh", "y", "zl"), 0, 0, tiled=True
    ).reshape(MIXED, D)
    grads = call(
        weight_grad_kernel,
        [((D, UNITS), F32), ((UNITS, D), F32)] + [((PACKED, UNITS), BF)] * (X - 1),
        *own[2:], *other[2:], returned,
        in_specs=[vmem] * 8 + [pl.BlockSpec(memory_space=pl.ANY)],
    )
    arrived = [shift(grads[1 + k], "x", X, k) for k in range(1, X)]
    first_grad, second_grad = call(
        total_kernel, [((1, D, UNITS), F32), ((1, UNITS, D), F32)], *grads[:2], *arrived
    )
    centroid_grad += shift(centroid_grad, "zh", ZH, 1)
    grad_centroid = centroid_grad + sum(shift(centroid_grad, "x", X, k) for k in range(1, X))
    layer_out, grad_tokens = call(
        unpack_kernel, [((TOK, D), BF), ((TOK, D), BF)], slot_order, home, tokens, out_grad
    )
    return (layer_out, grad_tokens, grad_centroid, first_grad, second_grad)


def solution(mesh):
    fine = Mesh(mesh.devices.reshape(ZH, X, CORE, Y, ZL), ("zh", "x", "core", "y", "zl"))
    dp, expert = ("zh", "x", "core"), ("y", "zl")
    both = dp + expert
    placed = (
        P(both, None),
        P(both, None),
        P(expert, None),
        P(expert, None, dp),
        P(expert, dp, None),
        P(both, None),
    )
    return jax.shard_map(
        on_device,
        mesh=fine,
        in_specs=placed,
        out_specs=(
            P(both, None),
            P(both, None),
            P(expert, None),
            P(expert, None, dp),
            P(expert, dp, None),
        ),
        check_vma=False,
    )
```

```python
import math

import jax
import jax.numpy as jnp
from jax import lax
from jax.experimental import pallas as pl
from jax.experimental.pallas import tpu as pltpu
from jax.sharding import Mesh
from jax.sharding import PartitionSpec as P

BF = jnp.bfloat16
F32 = jnp.float32
ZH, X, CORE, Y, ZL = 2, 4, 2, 4, 8
EXPERTS = Y * ZL
BLK = 4
D = 512
TOK = EXPERTS * BLK
ROWS = ZH * TOK
MIXED = 2 * ROWS
UNITS = 256
HALF = D // 2
PACKED = D + 2 * UNITS
HID, DHID, ROUTED, DEXP, KEPT = 0, X * UNITS, 2 * X * UNITS, 2 * X * UNITS + D, 2 * X * UNITS + 2 * D
NOTE = 16
VMEM_LIMIT = 16 * 1024 * 1024


def dot(a, b, ca=1, cb=0):
    return lax.dot_general(a, b, (((ca,), (cb,)), ((), ())), preferred_element_type=F32)


def iota(shape, axis):
    return lax.broadcasted_iota(jnp.int32, shape, axis)


def mixed_picks(rows, on_rows_first):
    shape = (rows, 2 * rows) if on_rows_first else (2 * rows, rows)
    plain = iota(shape, 0 if on_rows_first else 1)
    mixed = iota(shape, 1 if on_rows_first else 0)
    place = (plain // BLK) * (2 * BLK) + plain % BLK
    return (mixed == place).astype(BF), (mixed == place + BLK).astype(BF)


def pack_kernel(
    order_ref, tok_ref, grad_ref, out_ref, order_vmem, tok_vmem, grad_vmem, sems
):
    copies = [
        pltpu.make_async_copy(source, target, sems.at[i])
        for i, (source, target) in enumerate(
            ((order_ref, order_vmem), (tok_ref, tok_vmem), (grad_ref, grad_vmem))
        )
    ]
    for copy in copies:
        copy.start()
    token_pick, grad_pick = mixed_picks(TOK, True)
    source = iota((TOK, 2 * TOK), 0).astype(F32)
    kind = (iota((TOK, 2 * TOK), 1) // BLK) % 2
    copies[0].wait()
    order = jnp.broadcast_to(order_vmem[...].astype(F32), (8, TOK)).astype(BF)
    token_source = dot(order, token_pick)[0:1]
    grad_source = dot(order, grad_pick)[0:1]
    pick_token = ((source == token_source) & (kind == 0)).astype(BF)
    pick_grad = ((source == grad_source) & (kind == 1)).astype(BF)
    copies[1].wait()
    mixed = dot(pick_token, tok_vmem[...], 0, 0)
    copies[2].wait()
    mixed = (mixed + dot(pick_grad, grad_vmem[...], 0, 0)).astype(BF)
    for half in range(ZH):
        out_ref[half * 2 * TOK : (half + 1) * 2 * TOK, :] = mixed


def expert_kernel(
    rows_ref, centroid_ref, before_ref, s0, s1, s2, s3,
    mixed_ref, centroid_grad_ref, kept_ref, kept, sems,
):
    def keep(value, at, slot):
        columns = slice(at, at + value.shape[1])
        kept[:, columns] = value
        copies.append(
            pltpu.make_async_copy(kept.at[:, columns], kept_ref.at[:, columns], sems.at[slot])
        )
        copies[-1].start()

    copies = []
    token_pick, grad_pick = mixed_picks(ROWS, True)
    received = rows_ref[...]
    routed = dot(token_pick, received)
    d_routed = dot(grad_pick, received)
    centroid = centroid_ref[...].astype(F32)
    gating = jax.nn.sigmoid(jnp.sum(routed * centroid, axis=1, keepdims=True))
    routed_half = routed.astype(BF)
    d_expert = (gating * d_routed).astype(BF)
    keep(routed_half, ROUTED, 0)
    keep(d_expert, DEXP, 1)
    out_part = jnp.zeros((ROWS, D), F32)
    inner_part = jnp.zeros((ROWS, D), F32)
    scale = math.sqrt(2.0 / math.pi)
    d_expert_a, d_expert_b = d_expert[:, :HALF], d_expert[:, HALF:]
    for k, shard in enumerate((s0, s1, s2, s3)):
        w = shard[:D, :]
        v_a, v_b = shard[D : D + UNITS, :], shard[D + UNITS :, :]
        pre = dot(routed_half, w)
        square = pre * pre
        bend = jnp.tanh(scale * pre * (1.0 + 0.044715 * square))
        half_up = 0.5 * (1.0 + bend)
        hidden = (pre * half_up).astype(BF)
        slope = half_up + 0.5 * pre * (1.0 - bend * bend) * (
            scale * (1.0 + 3.0 * 0.044715 * square)
        )
        back = dot(d_expert_a, v_a, 1, 1) + dot(d_expert_b, v_b, 1, 1)
        d_hidden = (back * slope).astype(BF)
        out_part += jnp.concatenate([dot(hidden, v_a), dot(hidden, v_b)], axis=1)
        inner_part += dot(d_hidden, w, 1, 1)
        keep(hidden, HID + k * UNITS, 2 + 2 * k)
        keep(d_hidden, DHID + k * UNITS, 3 + 2 * k)
    d_logit = jnp.sum(d_routed * out_part, axis=1, keepdims=True) * gating * (1.0 - gating)
    centroid_grad = before_ref[...] + jnp.sum(d_logit * routed, axis=0, keepdims=True)
    centroid_grad_ref[...] = centroid_grad
    layer_part = (gating * out_part).astype(BF)
    grad_part = (inner_part + d_logit * centroid).astype(BF)
    token_place, grad_place = mixed_picks(ROWS, False)
    mixed_ref[...] = (dot(token_place, layer_part) + dot(grad_place, grad_part)).astype(BF)
    for copy in copies:
        copy.wait()


def join_kernel(own_ref, other_ref, here_ref, there_ref, out_ref, centroid_grad_ref):
    out_ref[...] = (own_ref[...].astype(F32) + other_ref[...].astype(F32)).astype(BF)
    centroid_grad_ref[...] = here_ref[...] + there_ref[...]


def weight_grad_kernel(
    kept_a_ref, kept_b_ref, here_ref, there_ref,
    own_in, own_out, own_centroid, p1, p2, p3, kept_a, kept_b, sems,
):
    copies = [
        pltpu.make_async_copy(kept_a_ref, kept_a, sems.at[0]),
        pltpu.make_async_copy(kept_b_ref, kept_b, sems.at[1]),
    ]
    for copy in copies:
        copy.start()
    centroid_grad = here_ref[...] + there_ref[...]
    own_centroid[...] = centroid_grad
    high = centroid_grad.astype(BF).astype(F32)
    row = iota((NOTE, D), 0)
    note = jnp.where(row == 0, high, jnp.where(row == 1, centroid_grad - high, 0.0)).astype(BF)
    for copy in copies:
        copy.wait()
    for k, packed in enumerate((None, p1, p2, p3)):
        units = slice(HID + k * UNITS, HID + (k + 1) * UNITS)
        d_units = slice(DHID + k * UNITS, DHID + (k + 1) * UNITS)
        first = dot(kept_a[:, ROUTED:DEXP], kept_a[:, d_units], 0, 0) + dot(
            kept_b[:, ROUTED:DEXP], kept_b[:, d_units], 0, 0
        )
        second = dot(kept_a[:, units], kept_a[:, DEXP:KEPT], 0, 0) + dot(
            kept_b[:, units], kept_b[:, DEXP:KEPT], 0, 0
        )
        if packed is None:
            own_in[...] = first
            own_out[...] = second
        else:
            packed[:D, :] = first.astype(BF)
            packed[D : D + UNITS, :] = second[:, :HALF].astype(BF)
            packed[D + UNITS : PACKED, :] = second[:, HALF:].astype(BF)
            packed[PACKED : PACKED + NOTE, :] = note[:, :HALF]
            packed[PACKED + NOTE :, :] = note[:, HALF:]


def total_kernel(
    own_in, own_out, own_centroid, p1, p2, p3, first_ref, second_ref, centroid_grad_ref
):
    def total(rows):
        return p1[rows, :].astype(F32) + p2[rows, :].astype(F32) + p3[rows, :].astype(F32)

    def note(at):
        rows = total(slice(at, at + NOTE))
        return rows[0:1] + rows[1:2]

    first_ref[0] = own_in[...] + total(slice(0, D))
    second_ref[0, :, :HALF] = own_out[:, :HALF] + total(slice(D, D + UNITS))
    second_ref[0, :, HALF:] = own_out[:, HALF:] + total(slice(D + UNITS, PACKED))
    centroid_grad_ref[:, :HALF] = own_centroid[:, :HALF] + note(PACKED)
    centroid_grad_ref[:, HALF:] = own_centroid[:, HALF:] + note(PACKED + NOTE)


def unpack_kernel(order_ref, home_ref, tok_ref, grad_ref, layer_ref, grad_out_ref):
    order = jnp.broadcast_to(order_ref[...].astype(F32), (8, TOK)).astype(BF)
    token = iota((TOK, 2 * TOK), 0).astype(F32)
    token_pick, grad_pick = mixed_picks(TOK, True)
    kind = (iota((TOK, 2 * TOK), 1) // BLK) % 2
    pick_token = ((token == dot(order, token_pick)[0:1]) & (kind == 0)).astype(BF)
    pick_grad = ((token == dot(order, grad_pick)[0:1]) & (kind == 1)).astype(BF)
    layer = tok_ref[...].astype(F32)
    grad = grad_ref[...].astype(F32)
    for half in range(ZH):
        rows = home_ref[half * 2 * TOK : (half + 1) * 2 * TOK, :]
        layer += dot(pick_token, rows)
        grad += dot(pick_grad, rows)
    layer_ref[...] = layer.astype(BF)
    grad_out_ref[...] = grad.astype(BF)


def in_hbm(value):
    return pltpu.with_memory_space_constraint(value, pltpu.HBM)


def call(kernel, outs, *operands, **options):
    return pl.pallas_call(
        kernel,
        out_shape=[
            out if hasattr(out, "memory_space") else jax.ShapeDtypeStruct(*out) for out in outs
        ],
        compiler_params=pltpu.CompilerParams(vmem_limit_bytes=VMEM_LIMIT),
        **options,
    )(*operands)


def shift(value, axis, size, by):
    return lax.ppermute(value, axis, [(i, (i + by) % size) for i in range(size)])


def on_device(tokens, slot_order, centroid, weight_in, weight_out, out_grad):
    vmem, hbm = pl.BlockSpec(memory_space=pltpu.VMEM), pl.BlockSpec(memory_space=pltpu.HBM)
    second = weight_out[0]
    shard = jnp.concatenate([weight_in[0], second[:, :HALF], second[:, HALF:]], axis=0)
    shards = [shard] + [shift(shard, "x", X, -k) for k in range(1, X)]
    (packed,) = call(
        pack_kernel,
        [((MIXED, D), BF)],
        *(in_hbm(each) for each in (slot_order, tokens, out_grad)),
        in_specs=[hbm] * 3,
        out_specs=[vmem],
        scratch_shapes=[
            pltpu.VMEM((1, TOK), jnp.int32),
            pltpu.VMEM((TOK, D), BF),
            pltpu.VMEM((TOK, D), BF),
            pltpu.SemaphoreType.DMA((3,)),
        ],
    )
    own_rows = lax.all_to_all(
        packed.reshape(ZH * EXPERTS, 2 * BLK, D), ("zh", "y", "zl"), 0, 0, tiled=True
    ).reshape(MIXED, D)
    other_rows = shift(own_rows, "core", CORE, 1)
    options = dict(
        in_specs=[vmem] * (3 + X),
        out_specs=[vmem, vmem, hbm],
        scratch_shapes=[pltpu.VMEM((ROWS, KEPT), BF), pltpu.SemaphoreType.DMA((2 + 2 * X,))],
    )
    outs = [((MIXED, D), BF), ((1, D), F32), pltpu.HBM((ROWS, KEPT), BF)]
    nothing = jnp.zeros((1, D), F32)
    own = call(expert_kernel, outs, own_rows, centroid, nothing, *shards, **options)
    other = call(expert_kernel, outs, other_rows, centroid, own[1], *shards, **options)
    from_other = shift(other[0], "core", CORE, 1)
    returned, centroid_term = call(
        join_kernel,
        [((MIXED, D), BF), ((1, D), F32)],
        own[0], from_other, other[1], shift(other[1], "zh", ZH, 1),
    )
    home = lax.all_to_all(
        returned.reshape(ZH * EXPERTS, 2 * BLK, D), ("zh", "y", "zl"), 0, 0, tiled=True
    ).reshape(MIXED, D)
    grads = call(
        weight_grad_kernel,
        [((D, UNITS), F32), ((UNITS, D), F32), ((1, D), F32)]
        + [((PACKED + 2 * NOTE, UNITS), BF)] * (X - 1),
        in_hbm(own[2]), in_hbm(other[2]), centroid_term, shift(centroid_term, "core", CORE, 1),
        in_specs=[hbm, hbm, vmem, vmem],
        scratch_shapes=[
            pltpu.VMEM((ROWS, KEPT), BF), pltpu.VMEM((ROWS, KEPT), BF),
            pltpu.SemaphoreType.DMA((2,)),
        ],
    )
    arrived = [shift(grads[2 + k], "x", X, k) for k in range(1, X)]
    first_grad, second_grad, grad_centroid = call(
        total_kernel,
        [((1, D, UNITS), F32), ((1, UNITS, D), F32), ((1, D), F32)],
        *grads[:3], *arrived,
    )
    layer_out, grad_tokens = call(
        unpack_kernel, [((TOK, D), BF), ((TOK, D), BF)], slot_order, home, tokens, out_grad
    )
    return (layer_out, grad_tokens, grad_centroid, first_grad, second_grad)


def solution(mesh):
    fine = Mesh(mesh.devices.reshape(ZH, X, CORE, Y, ZL), ("zh", "x", "core", "y", "zl"))
    dp, expert = ("zh", "x", "core"), ("y", "zl")
    both = dp + expert
    placed = (
        P(both, None),
        P(both, None),
        P(expert, None),
        P(expert, None, dp),
        P(expert, dp, None),
        P(both, None),
    )
    return jax.shard_map(
        on_device,
        mesh=fine,
        in_specs=placed,
        out_specs=(
            P(both, None),
            P(both, None),
            P(expert, None),
            P(expert, None, dp),
            P(expert, dp, None),
        ),
        check_vma=False,
    )
```

```python
import math

import jax
import jax.numpy as jnp
from jax import lax
from jax.experimental import pallas as pl
from jax.experimental.pallas import tpu as pltpu
from jax.sharding import Mesh
from jax.sharding import PartitionSpec as P

BF = jnp.bfloat16
F32 = jnp.float32
ZH, X, CORE, Y, ZL = 2, 4, 2, 4, 8
EXPERTS = Y * ZL
BLK = 4
D = 512
TOK = EXPERTS * BLK
ROWS = ZH * TOK
MIXED = 2 * ROWS
UNITS = 256
HALF = D // 2
PACKED = D + 2 * UNITS
SHARDS = X * CORE
VMEM_LIMIT = 16 * 1024 * 1024


def dot(a, b, ca=1, cb=0):
    return lax.dot_general(a, b, (((ca,), (cb,)), ((), ())), preferred_element_type=F32)


def iota(shape, axis):
    return lax.broadcasted_iota(jnp.int32, shape, axis)


def mixed_picks(rows, on_rows_first):
    shape = (rows, 2 * rows) if on_rows_first else (2 * rows, rows)
    plain = iota(shape, 0 if on_rows_first else 1)
    mixed = iota(shape, 1 if on_rows_first else 0)
    place = (plain // BLK) * (2 * BLK) + plain % BLK
    return (mixed == place).astype(BF), (mixed == place + BLK).astype(BF)


def pack_kernel(
    order_ref, tok_ref, grad_ref, first_ref, second_ref,
    out_ref, shard_ref, order_vmem, tok_vmem, grad_vmem, shard_vmem, sems,
):
    copies = [
        pltpu.make_async_copy(source, target, sems.at[i])
        for i, (source, target) in enumerate(
            (
                (order_ref, order_vmem),
                (tok_ref, tok_vmem),
                (grad_ref, grad_vmem),
                (first_ref.at[0], shard_vmem.at[:D, :]),
                (second_ref.at[0, :, :HALF], shard_vmem.at[D : D + UNITS, :]),
                (second_ref.at[0, :, HALF:], shard_vmem.at[D + UNITS :, :]),
            )
        )
    ]
    for copy in copies:
        copy.start()
    for copy in copies[3:]:
        copy.wait()
    shard_out = pltpu.make_async_copy(shard_vmem, shard_ref, sems.at[6])
    shard_out.start()
    token_pick, grad_pick = mixed_picks(TOK, True)
    copies[0].wait()
    order = jnp.broadcast_to(order_vmem[...].astype(F32), (8, TOK)).astype(BF)
    source = iota((TOK, 2 * TOK), 0).astype(F32)
    token_source = dot(order, token_pick)[0:1]
    grad_source = dot(order, grad_pick)[0:1]
    kind = (iota((TOK, 2 * TOK), 1) // BLK) % 2
    pick_token = ((source == token_source) & (kind == 0)).astype(BF)
    pick_grad = ((source == grad_source) & (kind == 1)).astype(BF)
    copies[1].wait()
    mixed = dot(pick_token, tok_vmem[...], 0, 0)
    copies[2].wait()
    mixed = (mixed + dot(pick_grad, grad_vmem[...], 0, 0)).astype(BF)
    for half in range(ZH):
        out_ref[half * 2 * TOK : (half + 1) * 2 * TOK, :] = mixed
    shard_out.wait()


def expert_kernel(
    rows_ref, centroid_ref, shards_ref,
    mixed_ref, centroid_grad_ref, routed_ref, d_expert_ref, hidden_ref, d_hidden_ref,
    shards_vmem, centroid_vmem, sems,
):
    centroid_copy = pltpu.make_async_copy(centroid_ref, centroid_vmem, sems.at[SHARDS])
    centroid_copy.start()
    copies = [
        pltpu.make_async_copy(
            shards_ref.at[k * PACKED : (k + 1) * PACKED, :], shards_vmem.at[k], sems.at[k]
        )
        for k in range(SHARDS)
    ]
    for copy in copies:
        copy.start()
    token_pick, grad_pick = mixed_picks(ROWS, True)
    received = rows_ref[...]
    routed = dot(token_pick, received)
    d_routed = dot(grad_pick, received)
    centroid_copy.wait()
    centroid = centroid_vmem[...].astype(F32)
    gating = jax.nn.sigmoid(jnp.sum(routed * centroid, axis=1, keepdims=True))
    routed_half = routed.astype(BF)
    d_expert = (gating * d_routed).astype(BF)
    routed_ref[...] = routed_half
    d_expert_ref[...] = d_expert
    d_expert_a, d_expert_b = d_expert[:, :HALF], d_expert[:, HALF:]
    out_part = jnp.zeros((ROWS, D), F32)
    inner_part = jnp.zeros((ROWS, D), F32)
    scale = math.sqrt(2.0 / math.pi)
    for k in range(SHARDS):
        copies[k].wait()
        w = shards_vmem[k, :D, :]
        v_a, v_b = shards_vmem[k, D : D + UNITS, :], shards_vmem[k, D + UNITS :, :]
        pre = dot(routed_half, w)
        square = pre * pre
        bend = jnp.tanh(scale * pre * (1.0 + 0.044715 * square))
        half_up = 0.5 * (1.0 + bend)
        hidden = (pre * half_up).astype(BF)
        slope = half_up + 0.5 * pre * (1.0 - bend * bend) * (
            scale * (1.0 + 3.0 * 0.044715 * square)
        )
        back = dot(d_expert_a, v_a, 1, 1) + dot(d_expert_b, v_b, 1, 1)
        d_hidden = (back * slope).astype(BF)
        out_part += jnp.concatenate([dot(hidden, v_a), dot(hidden, v_b)], axis=1)
        inner_part += dot(d_hidden, w, 1, 1)
        hidden_ref[:, k * UNITS : (k + 1) * UNITS] = hidden
        d_hidden_ref[:, k * UNITS : (k + 1) * UNITS] = d_hidden
    d_logit = jnp.sum(d_routed * out_part, axis=1, keepdims=True) * gating * (1.0 - gating)
    centroid_grad_ref[...] = jnp.sum(d_logit * routed, axis=0, keepdims=True)
    layer_part = (gating * out_part).astype(BF)
    grad_part = (inner_part + d_logit * centroid).astype(BF)
    token_place, grad_place = mixed_picks(ROWS, False)
    mixed_ref[...] = (dot(token_place, layer_part) + dot(grad_place, grad_part)).astype(BF)


def weight_grad_kernel(
    routed_ref, d_expert_ref, hidden_ref, d_hidden_ref, packed_ref, packed_vmem, sems
):
    copies = []
    for k in range(SHARDS):
        units = slice(k * UNITS, (k + 1) * UNITS)
        first = dot(routed_ref[...], d_hidden_ref[:, units], 0, 0)
        second = dot(hidden_ref[:, units], d_expert_ref[...], 0, 0)
        packed_vmem[k, :D, :] = first.astype(BF)
        packed_vmem[k, D : D + UNITS, :] = second[:, :HALF].astype(BF)
        packed_vmem[k, D + UNITS :, :] = second[:, HALF:].astype(BF)
        copies.append(
            pltpu.make_async_copy(
                packed_vmem.at[k], packed_ref.at[k * PACKED : (k + 1) * PACKED, :], sems.at[k]
            )
        )
        copies[k].start()
    for copy in copies:
        copy.wait()


def spread_kernel(grads_ref, first_ref, second_ref, packed_ref, sem):
    copy = pltpu.make_async_copy(grads_ref, packed_ref, sem)
    copy.start()
    copy.wait()
    first_ref[0] = packed_ref[:D, :].astype(F32)
    second_ref[0, :, :HALF] = packed_ref[D : D + UNITS, :].astype(F32)
    second_ref[0, :, HALF:] = packed_ref[D + UNITS :, :].astype(F32)


def unpack_kernel(order_ref, home_ref, tok_ref, grad_ref, layer_ref, grad_out_ref):
    order = jnp.broadcast_to(order_ref[...].astype(F32), (8, TOK)).astype(BF)
    token = iota((TOK, 2 * TOK), 0).astype(F32)
    token_pick, grad_pick = mixed_picks(TOK, True)
    kind = (iota((TOK, 2 * TOK), 1) // BLK) % 2
    pick_token = ((token == dot(order, token_pick)[0:1]) & (kind == 0)).astype(BF)
    pick_grad = ((token == dot(order, grad_pick)[0:1]) & (kind == 1)).astype(BF)
    layer = tok_ref[...].astype(F32)
    grad = grad_ref[...].astype(F32)
    for half in range(ZH):
        rows = home_ref[half * 2 * TOK : (half + 1) * 2 * TOK, :]
        layer += dot(pick_token, rows)
        grad += dot(pick_grad, rows)
    layer_ref[...] = layer.astype(BF)
    grad_out_ref[...] = grad.astype(BF)


def in_hbm(value):
    return pltpu.with_memory_space_constraint(value, pltpu.HBM)


def hbm_out(shape, dtype):
    return pltpu.HBM(shape, dtype)


def call(kernel, outs, *operands, **options):
    return pl.pallas_call(
        kernel,
        out_shape=[
            out if hasattr(out, "memory_space") else jax.ShapeDtypeStruct(*out) for out in outs
        ],
        compiler_params=pltpu.CompilerParams(vmem_limit_bytes=VMEM_LIMIT),
        **options,
    )(*operands)


def shift(value, axis, size, by):
    return lax.ppermute(value, axis, [(i, (i + by) % size) for i in range(size)])


def on_device(tokens, slot_order, centroid, weight_in, weight_out, out_grad):
    vmem, hbm = pl.BlockSpec(memory_space=pltpu.VMEM), pl.BlockSpec(memory_space=pltpu.HBM)
    packed, shard = call(
        pack_kernel,
        [((MIXED, D), BF), hbm_out((PACKED, UNITS), BF)],
        *(in_hbm(each) for each in (slot_order, tokens, out_grad, weight_in, weight_out)),
        in_specs=[hbm] * 5,
        out_specs=[vmem, hbm],
        scratch_shapes=[
            pltpu.VMEM((1, TOK), jnp.int32),
            pltpu.VMEM((TOK, D), BF),
            pltpu.VMEM((TOK, D), BF),
            pltpu.VMEM((PACKED, UNITS), BF),
            pltpu.SemaphoreType.DMA((7,)),
        ],
    )
    shards = lax.all_gather(shard, ("x", "core"), axis=0, tiled=True)
    rows = lax.all_to_all(
        packed.reshape(ZH * EXPERTS, 2 * BLK, D), ("zh", "y", "zl"), 0, 0, tiled=True
    ).reshape(MIXED, D)
    mixed, centroid_term, *kept = call(
        expert_kernel,
        [
            ((MIXED, D), BF), ((1, D), F32), ((ROWS, D), BF), ((ROWS, D), BF),
            ((ROWS, SHARDS * UNITS), BF), ((ROWS, SHARDS * UNITS), BF),
        ],
        rows, in_hbm(centroid), in_hbm(shards),
        in_specs=[vmem, hbm, hbm],
        out_specs=[vmem] * 6,
        scratch_shapes=[
            pltpu.VMEM((SHARDS, PACKED, UNITS), BF),
            pltpu.VMEM((1, D), BF),
            pltpu.SemaphoreType.DMA((SHARDS + 1,)),
        ],
    )
    home = lax.all_to_all(
        mixed.reshape(ZH * EXPERTS, 2 * BLK, D), ("zh", "y", "zl"), 0, 0, tiled=True
    ).reshape(MIXED, D)
    (packed_grads,) = call(
        weight_grad_kernel,
        [hbm_out((SHARDS * PACKED, UNITS), BF)],
        *kept,
        in_specs=[vmem] * 4,
        out_specs=[hbm],
        scratch_shapes=[
            pltpu.VMEM((SHARDS, PACKED, UNITS), BF), pltpu.SemaphoreType.DMA((SHARDS,)),
        ],
    )
    grads = lax.psum_scatter(packed_grads, ("x", "core"), scatter_dimension=0, tiled=True)
    first_grad, second_grad = call(
        spread_kernel,
        [((1, D, UNITS), F32), ((1, UNITS, D), F32)],
        in_hbm(grads),
        in_specs=[hbm],
        out_specs=[vmem, vmem],
        scratch_shapes=[pltpu.VMEM((PACKED, UNITS), BF), pltpu.SemaphoreType.DMA(())],
    )
    centroid_term += shift(centroid_term, "zh", ZH, 1)
    centroid_term += shift(centroid_term, "core", CORE, 1)
    grad_centroid = centroid_term + sum(shift(centroid_term, "x", X, k) for k in range(1, X))
    layer_out, grad_tokens = call(
        unpack_kernel, [((TOK, D), BF), ((TOK, D), BF)], slot_order, home, tokens, out_grad
    )
    return (layer_out, grad_tokens, grad_centroid, first_grad, second_grad)


def solution(mesh):
    fine = Mesh(mesh.devices.reshape(ZH, X, CORE, Y, ZL), ("zh", "x", "core", "y", "zl"))
    dp, expert = ("zh", "x", "core"), ("y", "zl")
    both = dp + expert
    placed = (
        P(both, None),
        P(both, None),
        P(expert, None),
        P(expert, None, dp),
        P(expert, dp, None),
        P(both, None),
    )
    return jax.shard_map(
        on_device,
        mesh=fine,
        in_specs=placed,
        out_specs=(
            P(both, None),
            P(both, None),
            P(expert, None),
            P(expert, None, dp),
            P(expert, dp, None),
        ),
        check_vma=False,
    )
```

```python
import math

import jax
import jax.numpy as jnp
from jax import lax
from jax.experimental import pallas as pl
from jax.experimental.pallas import tpu as pltpu
from jax.sharding import Mesh
from jax.sharding import PartitionSpec as P

BF = jnp.bfloat16
F32 = jnp.float32
ZH, X, CORE, Y, ZL = 2, 4, 2, 4, 8
EXPERTS = Y * ZL
BLK = 4
D = 512
TOK = EXPERTS * BLK
ROWS = ZH * TOK
MIXED = 2 * ROWS
UNITS = 256
HALF = D // 2
PACKED = D + 2 * UNITS
NOTE = 16
VMEM_LIMIT = 16 * 1024 * 1024


def dot(a, b, ca=1, cb=0):
    return lax.dot_general(a, b, (((ca,), (cb,)), ((), ())), preferred_element_type=F32)


def iota(shape, axis):
    return lax.broadcasted_iota(jnp.int32, shape, axis)


def mixed_picks(rows, on_rows_first):
    shape = (rows, 2 * rows) if on_rows_first else (2 * rows, rows)
    plain = iota(shape, 0 if on_rows_first else 1)
    mixed = iota(shape, 1 if on_rows_first else 0)
    place = (plain // BLK) * (2 * BLK) + plain % BLK
    return (mixed == place).astype(BF), (mixed == place + BLK).astype(BF)


def pack_kernel(
    order_ref, tok_ref, grad_ref, out_ref, order_vmem, tok_vmem, grad_vmem, sems
):
    copies = [
        pltpu.make_async_copy(source, target, sems.at[i])
        for i, (source, target) in enumerate(
            ((order_ref, order_vmem), (tok_ref, tok_vmem), (grad_ref, grad_vmem))
        )
    ]
    for copy in copies:
        copy.start()
    token_pick, grad_pick = mixed_picks(TOK, True)
    source = iota((TOK, 2 * TOK), 0).astype(F32)
    kind = (iota((TOK, 2 * TOK), 1) // BLK) % 2
    copies[0].wait()
    order = jnp.broadcast_to(order_vmem[...].astype(F32), (8, TOK)).astype(BF)
    token_source = dot(order, token_pick)[0:1]
    grad_source = dot(order, grad_pick)[0:1]
    pick_token = ((source == token_source) & (kind == 0)).astype(BF)
    pick_grad = ((source == grad_source) & (kind == 1)).astype(BF)
    copies[1].wait()
    mixed = dot(pick_token, tok_vmem[...], 0, 0)
    copies[2].wait()
    mixed = (mixed + dot(pick_grad, grad_vmem[...], 0, 0)).astype(BF)
    for half in range(ZH):
        out_ref[half * 2 * TOK : (half + 1) * 2 * TOK, :] = mixed


def expert_kernel(
    rows_ref, centroid_ref, before_ref, s0, s1, s2, s3,
    mixed_ref, centroid_grad_ref, routed_ref, d_expert_ref, hidden_ref, d_hidden_ref,
):
    token_pick, grad_pick = mixed_picks(ROWS, True)
    received = rows_ref[...]
    routed = dot(token_pick, received)
    d_routed = dot(grad_pick, received)
    centroid = centroid_ref[...].astype(F32)
    gating = jax.nn.sigmoid(jnp.sum(routed * centroid, axis=1, keepdims=True))
    routed_half = routed.astype(BF)
    d_expert = (gating * d_routed).astype(BF)
    routed_ref[...] = routed_half
    d_expert_ref[...] = d_expert
    out_part = jnp.zeros((ROWS, D), F32)
    inner_part = jnp.zeros((ROWS, D), F32)
    scale = math.sqrt(2.0 / math.pi)
    d_expert_a, d_expert_b = d_expert[:, :HALF], d_expert[:, HALF:]
    for k, shard in enumerate((s0, s1, s2, s3)):
        w = shard[:D, :]
        v_a, v_b = shard[D : D + UNITS, :], shard[D + UNITS :, :]
        pre = dot(routed_half, w)
        square = pre * pre
        bend = jnp.tanh(scale * pre * (1.0 + 0.044715 * square))
        half_up = 0.5 * (1.0 + bend)
        hidden = (pre * half_up).astype(BF)
        slope = half_up + 0.5 * pre * (1.0 - bend * bend) * (
            scale * (1.0 + 3.0 * 0.044715 * square)
        )
        back = dot(d_expert_a, v_a, 1, 1) + dot(d_expert_b, v_b, 1, 1)
        d_hidden = (back * slope).astype(BF)
        out_part += jnp.concatenate([dot(hidden, v_a), dot(hidden, v_b)], axis=1)
        inner_part += dot(d_hidden, w, 1, 1)
        hidden_ref[:, k * UNITS : (k + 1) * UNITS] = hidden
        d_hidden_ref[:, k * UNITS : (k + 1) * UNITS] = d_hidden
    d_logit = jnp.sum(d_routed * out_part, axis=1, keepdims=True) * gating * (1.0 - gating)
    centroid_grad = before_ref[...] + jnp.sum(d_logit * routed, axis=0, keepdims=True)
    centroid_grad_ref[...] = centroid_grad
    layer_part = (gating * out_part).astype(BF)
    grad_part = (inner_part + d_logit * centroid).astype(BF)
    token_place, grad_place = mixed_picks(ROWS, False)
    mixed_ref[...] = (dot(token_place, layer_part) + dot(grad_place, grad_part)).astype(BF)


def join_kernel(own_ref, other_ref, out_ref):
    out_ref[...] = (own_ref[...].astype(F32) + other_ref[...].astype(F32)).astype(BF)


def weight_grad_kernel(
    centroid_ref, routed_a, d_expert_a, hidden_a, d_hidden_a,
    routed_b, d_expert_b, hidden_b, d_hidden_b, after_ref, own_in_ref, own_out_ref, p1, p2, p3,
    own_in, own_out, sems,
):
    high = centroid_ref[...].astype(BF).astype(F32)
    row = iota((NOTE, D), 0)
    note = jnp.where(row == 0, high, jnp.where(row == 1, centroid_ref[...] - high, 0.0)).astype(BF)
    copies = [
        pltpu.make_async_copy(own_in, own_in_ref, sems.at[0]),
        pltpu.make_async_copy(own_out, own_out_ref, sems.at[1]),
    ]
    for k, packed in enumerate((None, p1, p2, p3)):
        units = slice(k * UNITS, (k + 1) * UNITS)
        first = dot(routed_a[...], d_hidden_a[:, units], 0, 0) + dot(
            routed_b[...], d_hidden_b[:, units], 0, 0
        )
        second = dot(hidden_a[:, units], d_expert_a[...], 0, 0) + dot(
            hidden_b[:, units], d_expert_b[...], 0, 0
        )
        if packed is None:
            own_in[...] = first
            own_out[...] = second
            for copy in copies:
                copy.start()
        else:
            packed[:D, :] = first.astype(BF)
            packed[D : D + UNITS, :] = second[:, :HALF].astype(BF)
            packed[D + UNITS : PACKED, :] = second[:, HALF:].astype(BF)
            packed[PACKED : PACKED + NOTE, :] = note[:, :HALF]
            packed[PACKED + NOTE :, :] = note[:, HALF:]
    for copy in copies:
        copy.wait()


def note_kernel(own_centroid, p1, p2, p3, out_ref):
    for at, columns in ((PACKED, slice(0, HALF)), (PACKED + NOTE, slice(HALF, D))):
        rows = slice(at, at + NOTE)
        notes = p1[rows, :].astype(F32) + p2[rows, :].astype(F32) + p3[rows, :].astype(F32)
        out_ref[:, columns] = own_centroid[:, columns] + notes[0:1] + notes[1:2]


def total_kernel(
    own_in_ref, own_out_ref, p1, p2, p3, first_ref, second_ref, own_in, own_out, sems
):
    def total(rows):
        return p1[rows, :].astype(F32) + p2[rows, :].astype(F32) + p3[rows, :].astype(F32)

    copies = [
        pltpu.make_async_copy(own_in_ref, own_in, sems.at[0]),
        pltpu.make_async_copy(own_out_ref, own_out, sems.at[1]),
    ]
    for copy in copies:
        copy.start()
    copies[0].wait()
    first_ref[0] = own_in[...] + total(slice(0, D))
    copies[1].wait()
    second_ref[0, :, :HALF] = own_out[:, :HALF] + total(slice(D, D + UNITS))
    second_ref[0, :, HALF:] = own_out[:, HALF:] + total(slice(D + UNITS, PACKED))


def unpack_kernel(order_ref, home_ref, tok_ref, grad_ref, layer_ref, grad_out_ref):
    order = jnp.broadcast_to(order_ref[...].astype(F32), (8, TOK)).astype(BF)
    token = iota((TOK, 2 * TOK), 0).astype(F32)
    token_pick, grad_pick = mixed_picks(TOK, True)
    kind = (iota((TOK, 2 * TOK), 1) // BLK) % 2
    pick_token = ((token == dot(order, token_pick)[0:1]) & (kind == 0)).astype(BF)
    pick_grad = ((token == dot(order, grad_pick)[0:1]) & (kind == 1)).astype(BF)
    layer = tok_ref[...].astype(F32)
    grad = grad_ref[...].astype(F32)
    for half in range(ZH):
        rows = home_ref[half * 2 * TOK : (half + 1) * 2 * TOK, :]
        layer += dot(pick_token, rows)
        grad += dot(pick_grad, rows)
    layer_ref[...] = layer.astype(BF)
    grad_out_ref[...] = grad.astype(BF)


def in_hbm(value):
    return pltpu.with_memory_space_constraint(value, pltpu.HBM)


def call(kernel, outs, *operands, **options):
    return pl.pallas_call(
        kernel,
        out_shape=[
            out if hasattr(out, "memory_space") else jax.ShapeDtypeStruct(*out) for out in outs
        ],
        compiler_params=pltpu.CompilerParams(vmem_limit_bytes=VMEM_LIMIT),
        **options,
    )(*operands)


def shift(value, axis, size, by):
    return lax.ppermute(value, axis, [(i, (i + by) % size) for i in range(size)])


def on_device(tokens, slot_order, centroid, weight_in, weight_out, out_grad):
    vmem, hbm = pl.BlockSpec(memory_space=pltpu.VMEM), pl.BlockSpec(memory_space=pltpu.HBM)
    second = weight_out[0]
    shard = jnp.concatenate([weight_in[0], second[:, :HALF], second[:, HALF:]], axis=0)
    shards = [shard] + [shift(shard, "x", X, -k) for k in range(1, X)]
    (packed,) = call(
        pack_kernel,
        [((MIXED, D), BF)],
        *(in_hbm(each) for each in (slot_order, tokens, out_grad)),
        in_specs=[hbm] * 3,
        out_specs=[vmem],
        scratch_shapes=[
            pltpu.VMEM((1, TOK), jnp.int32),
            pltpu.VMEM((TOK, D), BF),
            pltpu.VMEM((TOK, D), BF),
            pltpu.SemaphoreType.DMA((3,)),
        ],
    )
    own_rows = lax.all_to_all(
        packed.reshape(ZH * EXPERTS, 2 * BLK, D), ("zh", "y", "zl"), 0, 0, tiled=True
    ).reshape(MIXED, D)
    other_rows = shift(own_rows, "core", CORE, 1)
    part_shapes = [
        ((MIXED, D), BF), ((1, D), F32), ((ROWS, D), BF), ((ROWS, D), BF),
        ((ROWS, X * UNITS), BF), ((ROWS, X * UNITS), BF),
    ]
    nothing = jnp.zeros((1, D), F32)
    other = call(expert_kernel, part_shapes, other_rows, centroid, nothing, *shards)
    own = call(expert_kernel, part_shapes, own_rows, centroid, other[1], *shards)
    from_other = shift(other[0], "core", CORE, 1)
    own_scratch = [
        pltpu.VMEM((D, UNITS), F32), pltpu.VMEM((UNITS, D), F32), pltpu.SemaphoreType.DMA((2,)),
    ]
    grads = call(
        weight_grad_kernel,
        [pltpu.HBM((D, UNITS), F32), pltpu.HBM((UNITS, D), F32)]
        + [((PACKED + 2 * NOTE, UNITS), BF)] * (X - 1),
        *own[1:], *other[2:], from_other,
        in_specs=[vmem] * 9 + [pl.BlockSpec(memory_space=pl.ANY)],
        out_specs=[hbm, hbm] + [vmem] * (X - 1),
        scratch_shapes=own_scratch,
    )
    arrived = [shift(grads[1 + k], "x", X, k) for k in range(1, X)]
    (returned,) = call(join_kernel, [((MIXED, D), BF)], own[0], from_other)
    home = lax.all_to_all(
        returned.reshape(ZH * EXPERTS, 2 * BLK, D), ("zh", "y", "zl"), 0, 0, tiled=True
    ).reshape(MIXED, D)
    (centroid_grad,) = call(note_kernel, [((1, D), F32)], own[1], *arrived)
    centroid_grad += shift(centroid_grad, "core", CORE, 1)
    grad_centroid = centroid_grad + shift(centroid_grad, "zh", ZH, 1)
    first_grad, second_grad = call(
        total_kernel,
        [((1, D, UNITS), F32), ((1, UNITS, D), F32)],
        in_hbm(grads[0]), in_hbm(grads[1]), *arrived,
        in_specs=[hbm, hbm] + [vmem] * (X - 1),
        scratch_shapes=own_scratch,
        cost_estimate=pl.CostEstimate(flops=20 * 10**9, transcendentals=0, bytes_accessed=4 * 2**20),
    )
    layer_out, grad_tokens = call(
        unpack_kernel, [((TOK, D), BF), ((TOK, D), BF)], slot_order, home, tokens, out_grad
    )
    return (layer_out, grad_tokens, grad_centroid, first_grad, second_grad)


def solution(mesh):
    fine = Mesh(mesh.devices.reshape(ZH, X, CORE, Y, ZL), ("zh", "x", "core", "y", "zl"))
    dp, expert = ("zh", "x", "core"), ("y", "zl")
    both = dp + expert
    placed = (
        P(both, None),
        P(both, None),
        P(expert, None),
        P(expert, None, dp),
        P(expert, dp, None),
        P(both, None),
    )
    return jax.shard_map(
        on_device,
        mesh=fine,
        in_specs=placed,
        out_specs=(
            P(both, None),
            P(both, None),
            P(expert, None),
            P(expert, None, dp),
            P(expert, dp, None),
        ),
        check_vma=False,
    )
```

```python
import math

import jax
import jax.numpy as jnp
from jax import lax
from jax.experimental import pallas as pl
from jax.experimental.pallas import tpu as pltpu
from jax.sharding import Mesh
from jax.sharding import PartitionSpec as P

BF = jnp.bfloat16
F32 = jnp.float32
ZH, X, CORE, Y, ZL = 2, 4, 2, 4, 8
EXPERTS = Y * ZL
BLK = 4
D = 512
TOK = EXPERTS * BLK
ROWS = ZH * TOK
MIXED = 2 * ROWS
UNITS = 256
HALF = D // 2
PACKED = D + 2 * UNITS
NOTE = 16
VMEM_LIMIT = 16 * 1024 * 1024


def dot(a, b, ca=1, cb=0):
    return lax.dot_general(a, b, (((ca,), (cb,)), ((), ())), preferred_element_type=F32)


def iota(shape, axis):
    return lax.broadcasted_iota(jnp.int32, shape, axis)


def mixed_picks(rows, on_rows_first, slots=False):
    shape = (rows, 2 * rows) if on_rows_first else (2 * rows, rows)
    plain = iota(shape, 0 if on_rows_first else 1)
    mixed = iota(shape, 1 if on_rows_first else 0)
    group = plain // BLK
    if slots:
        group = (group % ZL) * Y + group // ZL
    place = group * (2 * BLK) + plain % BLK
    return (mixed == place).astype(BF), (mixed == place + BLK).astype(BF)


def pack_kernel(
    order_ref, tok_ref, grad_ref, out_ref, order_vmem, tok_vmem, grad_vmem, sems
):
    copies = [
        pltpu.make_async_copy(source, target, sems.at[i])
        for i, (source, target) in enumerate(
            ((order_ref, order_vmem), (tok_ref, tok_vmem), (grad_ref, grad_vmem))
        )
    ]
    for copy in copies:
        copy.start()
    token_pick, grad_pick = mixed_picks(TOK, True, slots=True)
    source = iota((TOK, 2 * TOK), 0).astype(F32)
    kind = (iota((TOK, 2 * TOK), 1) // BLK) % 2
    copies[0].wait()
    order = jnp.broadcast_to(order_vmem[...].astype(F32), (8, TOK)).astype(BF)
    token_source = dot(order, token_pick)[0:1]
    grad_source = dot(order, grad_pick)[0:1]
    pick_token = ((source == token_source) & (kind == 0)).astype(BF)
    pick_grad = ((source == grad_source) & (kind == 1)).astype(BF)
    copies[1].wait()
    mixed = dot(pick_token, tok_vmem[...], 0, 0)
    copies[2].wait()
    mixed = (mixed + dot(pick_grad, grad_vmem[...], 0, 0)).astype(BF)
    for half in range(ZH):
        out_ref[half * 2 * TOK : (half + 1) * 2 * TOK, :] = mixed


def expert_kernel(
    rows_ref, centroid_ref, before_ref, s0, s1, s2, s3,
    mixed_ref, centroid_grad_ref, routed_ref, d_expert_ref, hidden_ref, d_hidden_ref,
):
    token_pick, grad_pick = mixed_picks(ROWS, True)
    received = rows_ref[...]
    routed = dot(token_pick, received)
    d_routed = dot(grad_pick, received)
    centroid = centroid_ref[...].astype(F32)
    gating = jax.nn.sigmoid(jnp.sum(routed * centroid, axis=1, keepdims=True))
    routed_half = routed.astype(BF)
    d_expert = (gating * d_routed).astype(BF)
    routed_ref[...] = routed_half
    d_expert_ref[...] = d_expert
    out_part = jnp.zeros((ROWS, D), F32)
    inner_part = jnp.zeros((ROWS, D), F32)
    scale = math.sqrt(2.0 / math.pi)
    d_expert_a, d_expert_b = d_expert[:, :HALF], d_expert[:, HALF:]
    for k, shard in enumerate((s0, s1, s2, s3)):
        w = shard[:D, :]
        v_a, v_b = shard[D : D + UNITS, :], shard[D + UNITS :, :]
        pre = dot(routed_half, w)
        square = pre * pre
        bend = jnp.tanh(scale * pre * (1.0 + 0.044715 * square))
        half_up = 0.5 * (1.0 + bend)
        hidden = (pre * half_up).astype(BF)
        slope = half_up + 0.5 * pre * (1.0 - bend * bend) * (
            scale * (1.0 + 3.0 * 0.044715 * square)
        )
        back = dot(d_expert_a, v_a, 1, 1) + dot(d_expert_b, v_b, 1, 1)
        d_hidden = (back * slope).astype(BF)
        out_part += jnp.concatenate([dot(hidden, v_a), dot(hidden, v_b)], axis=1)
        inner_part += dot(d_hidden, w, 1, 1)
        hidden_ref[:, k * UNITS : (k + 1) * UNITS] = hidden
        d_hidden_ref[:, k * UNITS : (k + 1) * UNITS] = d_hidden
    d_logit = jnp.sum(d_routed * out_part, axis=1, keepdims=True) * gating * (1.0 - gating)
    centroid_grad = before_ref[...] + jnp.sum(d_logit * routed, axis=0, keepdims=True)
    centroid_grad_ref[...] = centroid_grad
    layer_part = (gating * out_part).astype(BF)
    grad_part = (inner_part + d_logit * centroid).astype(BF)
    token_place, grad_place = mixed_picks(ROWS, False)
    mixed_ref[...] = (dot(token_place, layer_part) + dot(grad_place, grad_part)).astype(BF)


def join_kernel(own_ref, other_ref, out_ref):
    out_ref[...] = (own_ref[...].astype(F32) + other_ref[...].astype(F32)).astype(BF)


def weight_grad_kernel(
    centroid_ref, routed_a, d_expert_a, hidden_a, d_hidden_a,
    routed_b, d_expert_b, hidden_b, d_hidden_b, after_ref, own_ref, p1, p2, p3, own, sem,
):
    high = centroid_ref[...].astype(BF).astype(F32)
    row = iota((NOTE, D), 0)
    note = jnp.where(row == 0, high, jnp.where(row == 1, centroid_ref[...] - high, 0.0)).astype(BF)
    copy = pltpu.make_async_copy(own, own_ref, sem)
    for k, packed in enumerate((own, p1, p2, p3)):
        units = slice(k * UNITS, (k + 1) * UNITS)
        first = dot(routed_a[...], d_hidden_a[:, units], 0, 0) + dot(
            routed_b[...], d_hidden_b[:, units], 0, 0
        )
        second = dot(hidden_a[:, units], d_expert_a[...], 0, 0) + dot(
            hidden_b[:, units], d_expert_b[...], 0, 0
        )
        packed[:D, :] = first.astype(BF)
        packed[D : D + UNITS, :] = second[:, :HALF].astype(BF)
        packed[D + UNITS : PACKED, :] = second[:, HALF:].astype(BF)
        if k == 0:
            copy.start()
        else:
            packed[PACKED : PACKED + NOTE, :] = note[:, :HALF]
            packed[PACKED + NOTE :, :] = note[:, HALF:]
    copy.wait()


def note_kernel(own_centroid, p1, p2, p3, out_ref):
    for at, columns in ((PACKED, slice(0, HALF)), (PACKED + NOTE, slice(HALF, D))):
        rows = slice(at, at + NOTE)
        notes = p1[rows, :].astype(F32) + p2[rows, :].astype(F32) + p3[rows, :].astype(F32)
        out_ref[:, columns] = own_centroid[:, columns] + notes[0:1] + notes[1:2]


def total_kernel(own_ref, p1, p2, p3, first_ref, second_ref, own, sem):
    copy = pltpu.make_async_copy(own_ref, own, sem)
    copy.start()
    copy.wait()

    def total(rows):
        return (own[rows, :].astype(F32) + p1[rows, :].astype(F32)) + (
            p2[rows, :].astype(F32) + p3[rows, :].astype(F32)
        )

    first_ref[0] = total(slice(0, D))
    second_ref[0, :, :HALF] = total(slice(D, D + UNITS))
    second_ref[0, :, HALF:] = total(slice(D + UNITS, PACKED))


def unpack_kernel(
    order_ref, home_ref, tok_ref, grad_ref, layer_ref, grad_out_ref, order_vmem, tok, grad_vmem, sems
):
    copies = [
        pltpu.make_async_copy(source, target, sems.at[i])
        for i, (source, target) in enumerate(
            ((order_ref, order_vmem), (tok_ref, tok), (grad_ref, grad_vmem))
        )
    ]
    for copy in copies:
        copy.start()
    copies[0].wait()
    order = jnp.broadcast_to(order_vmem[...].astype(F32), (8, TOK)).astype(BF)
    token = iota((TOK, 2 * TOK), 0).astype(F32)
    token_pick, grad_pick = mixed_picks(TOK, True, slots=True)
    kind = (iota((TOK, 2 * TOK), 1) // BLK) % 2
    pick_token = ((token == dot(order, token_pick)[0:1]) & (kind == 0)).astype(BF)
    pick_grad = ((token == dot(order, grad_pick)[0:1]) & (kind == 1)).astype(BF)
    copies[1].wait()
    copies[2].wait()
    layer = tok[...].astype(F32)
    grad = grad_vmem[...].astype(F32)
    for half in range(ZH):
        rows = home_ref[half * 2 * TOK : (half + 1) * 2 * TOK, :]
        layer += dot(pick_token, rows)
        grad += dot(pick_grad, rows)
    layer_ref[...] = layer.astype(BF)
    grad_out_ref[...] = grad.astype(BF)


def in_hbm(value):
    return pltpu.with_memory_space_constraint(value, pltpu.HBM)


def call(kernel, outs, *operands, **options):
    return pl.pallas_call(
        kernel,
        out_shape=[
            out if hasattr(out, "memory_space") else jax.ShapeDtypeStruct(*out) for out in outs
        ],
        compiler_params=pltpu.CompilerParams(vmem_limit_bytes=VMEM_LIMIT),
        **options,
    )(*operands)


def shift(value, axis, size, by):
    return lax.ppermute(value, axis, [(i, (i + by) % size) for i in range(size)])


def on_device(tokens, slot_order, centroid, weight_in, weight_out, out_grad):
    vmem, hbm = pl.BlockSpec(memory_space=pltpu.VMEM), pl.BlockSpec(memory_space=pltpu.HBM)
    second = weight_out[0]
    shard = jnp.concatenate([weight_in[0], second[:, :HALF], second[:, HALF:]], axis=0)
    shards = [shard] + [shift(shard, "x", X, -k) for k in range(1, X)]
    token_scratch = [
        pltpu.VMEM((1, TOK), jnp.int32),
        pltpu.VMEM((TOK, D), BF),
        pltpu.VMEM((TOK, D), BF),
        pltpu.SemaphoreType.DMA((3,)),
    ]
    (packed,) = call(
        pack_kernel,
        [((MIXED, D), BF)],
        *(in_hbm(each) for each in (slot_order, tokens, out_grad)),
        in_specs=[hbm] * 3,
        out_specs=[vmem],
        scratch_shapes=token_scratch,
    )
    own_rows = lax.all_to_all(
        packed.reshape(ZH * EXPERTS, 2 * BLK, D), ("zh", "zl", "y"), 0, 0, tiled=True
    ).reshape(MIXED, D)
    other_rows = shift(own_rows, "core", CORE, 1)
    part_shapes = [
        ((MIXED, D), BF), ((1, D), F32), ((ROWS, D), BF), ((ROWS, D), BF),
        ((ROWS, X * UNITS), BF), ((ROWS, X * UNITS), BF),
    ]
    nothing = jnp.zeros((1, D), F32)
    other = call(expert_kernel, part_shapes, other_rows, centroid, nothing, *shards)
    own = call(expert_kernel, part_shapes, own_rows, centroid, other[1], *shards)
    from_other = shift(other[0], "core", CORE, 1)
    own_scratch = [pltpu.VMEM((PACKED, UNITS), BF), pltpu.SemaphoreType.DMA(())]
    grads = call(
        weight_grad_kernel,
        [pltpu.HBM((PACKED, UNITS), BF)] + [((PACKED + 2 * NOTE, UNITS), BF)] * (X - 1),
        *own[1:], *other[2:], from_other,
        in_specs=[vmem] * 9 + [pl.BlockSpec(memory_space=pl.ANY)],
        out_specs=[hbm] + [vmem] * (X - 1),
        scratch_shapes=own_scratch,
    )
    arrived = [shift(grads[k], "x", X, k) for k in range(1, X)]
    (returned,) = call(join_kernel, [((MIXED, D), BF)], own[0], from_other)
    home = lax.all_to_all(
        returned.reshape(ZH * EXPERTS, 2 * BLK, D), ("zh", "zl", "y"), 0, 0, tiled=True
    ).reshape(MIXED, D)
    (centroid_grad,) = call(note_kernel, [((1, D), F32)], own[1], *arrived)
    centroid_grad += shift(centroid_grad, "core", CORE, 1)
    grad_centroid = centroid_grad + shift(centroid_grad, "zh", ZH, 1)
    first_grad, second_grad = call(
        total_kernel,
        [((1, D, UNITS), F32), ((1, UNITS, D), F32)],
        in_hbm(grads[0]), *arrived,
        in_specs=[hbm] + [vmem] * (X - 1),
        scratch_shapes=own_scratch,
        cost_estimate=pl.CostEstimate(flops=20 * 10**9, transcendentals=0, bytes_accessed=4 * 2**20),
    )
    layer_out, grad_tokens = call(
        unpack_kernel,
        [((TOK, D), BF), ((TOK, D), BF)],
        in_hbm(slot_order), home, in_hbm(tokens), in_hbm(out_grad),
        in_specs=[hbm, vmem, hbm, hbm],
        scratch_shapes=token_scratch,
    )
    return (layer_out, grad_tokens, grad_centroid, first_grad, second_grad)


def solution(mesh):
    fine = Mesh(mesh.devices.reshape(ZH, X, CORE, Y, ZL), ("zh", "x", "core", "y", "zl"))
    dp, expert = ("zh", "x", "core"), ("y", "zl")
    both = dp + expert
    placed = (
        P(both, None),
        P(both, None),
        P(expert, None),
        P(expert, None, dp),
        P(expert, dp, None),
        P(both, None),
    )
    return jax.shard_map(
        on_device,
        mesh=fine,
        in_specs=placed,
        out_specs=(
            P(both, None),
            P(both, None),
            P(expert, None),
            P(expert, None, dp),
            P(expert, dp, None),
        ),
        check_vma=False,
    )
```

```python
import functools
import math

import jax
import jax.numpy as jnp
from jax import lax
from jax.experimental import pallas as pl
from jax.experimental.pallas import tpu as pltpu
from jax.sharding import Mesh
from jax.sharding import PartitionSpec as P

BF = jnp.bfloat16
F32 = jnp.float32
ZH, X, CORE, Y, ZL = 2, 4, 2, 4, 8
EXPERTS = Y * ZL
BLK = 4
D = 512
TOK = EXPERTS * BLK
ROWS = ZH * TOK
MIXED = 2 * ROWS
UNITS = 256
HALF = D // 2
PACKED = D + 2 * UNITS
NOTE = 16
VMEM_LIMIT = 16 * 1024 * 1024


def dot(a, b, ca=1, cb=0):
    return lax.dot_general(a, b, (((ca,), (cb,)), ((), ())), preferred_element_type=F32)


def iota(shape, axis):
    return lax.broadcasted_iota(jnp.int32, shape, axis)


def mixed_picks(rows, on_rows_first, slots=False):
    shape = (rows, 2 * rows) if on_rows_first else (2 * rows, rows)
    plain = iota(shape, 0 if on_rows_first else 1)
    mixed = iota(shape, 1 if on_rows_first else 0)
    group = plain // BLK
    if slots:
        group = (group % ZL) * Y + group // ZL
    place = group * (2 * BLK) + plain % BLK
    return (mixed == place).astype(BF), (mixed == place + BLK).astype(BF)


def pack_kernel(
    order_ref, tok_ref, grad_ref, out_ref, order_vmem, tok_vmem, grad_vmem, sems
):
    copies = [
        pltpu.make_async_copy(source, target, sems.at[i])
        for i, (source, target) in enumerate(
            ((order_ref, order_vmem), (tok_ref, tok_vmem), (grad_ref, grad_vmem))
        )
    ]
    for copy in copies:
        copy.start()
    token_pick, grad_pick = mixed_picks(TOK, True, slots=True)
    source = iota((TOK, 2 * TOK), 0).astype(F32)
    kind = (iota((TOK, 2 * TOK), 1) // BLK) % 2
    copies[0].wait()
    order = jnp.broadcast_to(order_vmem[...].astype(F32), (8, TOK)).astype(BF)
    token_source = dot(order, token_pick)[0:1]
    grad_source = dot(order, grad_pick)[0:1]
    pick_token = ((source == token_source) & (kind == 0)).astype(BF)
    pick_grad = ((source == grad_source) & (kind == 1)).astype(BF)
    copies[1].wait()
    mixed = dot(pick_token, tok_vmem[...], 0, 0)
    copies[2].wait()
    mixed = (mixed + dot(pick_grad, grad_vmem[...], 0, 0)).astype(BF)
    for half in range(ZH):
        out_ref[half * 2 * TOK : (half + 1) * 2 * TOK, :] = mixed


def expert_kernel(
    rows_ref, centroid_ref, before_ref, s0, s1, s2, s3,
    mixed_ref, centroid_grad_ref, routed_ref, d_expert_ref, hidden_ref, d_hidden_ref,
):
    token_pick, grad_pick = mixed_picks(ROWS, True)
    received = rows_ref[...]
    routed = dot(token_pick, received)
    d_routed = dot(grad_pick, received)
    centroid = centroid_ref[...].astype(F32)
    gating = jax.nn.sigmoid(jnp.sum(routed * centroid, axis=1, keepdims=True))
    routed_half = routed.astype(BF)
    d_expert = (gating * d_routed).astype(BF)
    routed_ref[...] = routed_half
    d_expert_ref[...] = d_expert
    out_part = jnp.zeros((ROWS, D), F32)
    inner_part = jnp.zeros((ROWS, D), F32)
    scale = math.sqrt(2.0 / math.pi)
    d_expert_a, d_expert_b = d_expert[:, :HALF], d_expert[:, HALF:]
    for k, shard in enumerate((s0, s1, s2, s3)):
        w = shard[:D, :]
        v_a, v_b = shard[D : D + UNITS, :], shard[D + UNITS :, :]
        pre = dot(routed_half, w)
        square = pre * pre
        bend = jnp.tanh(scale * pre * (1.0 + 0.044715 * square))
        half_up = 0.5 * (1.0 + bend)
        hidden = (pre * half_up).astype(BF)
        slope = half_up + 0.5 * pre * (1.0 - bend * bend) * (
            scale * (1.0 + 3.0 * 0.044715 * square)
        )
        back = dot(d_expert_a, v_a, 1, 1) + dot(d_expert_b, v_b, 1, 1)
        d_hidden = (back * slope).astype(BF)
        out_part += jnp.concatenate([dot(hidden, v_a), dot(hidden, v_b)], axis=1)
        inner_part += dot(d_hidden, w, 1, 1)
        hidden_ref[:, k * UNITS : (k + 1) * UNITS] = hidden
        d_hidden_ref[:, k * UNITS : (k + 1) * UNITS] = d_hidden
    d_logit = jnp.sum(d_routed * out_part, axis=1, keepdims=True) * gating * (1.0 - gating)
    centroid_grad = before_ref[...] + jnp.sum(d_logit * routed, axis=0, keepdims=True)
    centroid_grad_ref[...] = centroid_grad
    layer_part = (gating * out_part).astype(BF)
    grad_part = (inner_part + d_logit * centroid).astype(BF)
    token_place, grad_place = mixed_picks(ROWS, False)
    mixed_ref[...] = (dot(token_place, layer_part) + dot(grad_place, grad_part)).astype(BF)


def join_kernel(own_ref, other_ref, out_ref):
    out_ref[...] = (own_ref[...].astype(F32) + other_ref[...].astype(F32)).astype(BF)


def weight_grad_kernel(
    shards, centroid_ref, routed_a, d_expert_a, hidden_a, d_hidden_a,
    routed_b, d_expert_b, hidden_b, d_hidden_b, after_ref, *packed_refs,
):
    high = centroid_ref[...].astype(BF).astype(F32)
    row = iota((NOTE, D), 0)
    note = jnp.where(row == 0, high, jnp.where(row == 1, centroid_ref[...] - high, 0.0)).astype(BF)
    for k, packed in zip(shards, packed_refs):
        units = slice(k * UNITS, (k + 1) * UNITS)
        first = dot(routed_a[...], d_hidden_a[:, units], 0, 0) + dot(
            routed_b[...], d_hidden_b[:, units], 0, 0
        )
        second = dot(hidden_a[:, units], d_expert_a[...], 0, 0) + dot(
            hidden_b[:, units], d_expert_b[...], 0, 0
        )
        packed[:D, :] = first.astype(BF)
        packed[D : D + UNITS, :] = second[:, :HALF].astype(BF)
        packed[D + UNITS : PACKED, :] = second[:, HALF:].astype(BF)
        packed[PACKED : PACKED + NOTE, :] = note[:, :HALF]
        packed[PACKED + NOTE :, :] = note[:, HALF:]


def note_kernel(own_centroid, p1, p2, p3, out_ref):
    for at, columns in ((PACKED, slice(0, HALF)), (PACKED + NOTE, slice(HALF, D))):
        rows = slice(at, at + NOTE)
        notes = p1[rows, :].astype(F32) + p2[rows, :].astype(F32) + p3[rows, :].astype(F32)
        out_ref[:, columns] = own_centroid[:, columns] + notes[0:1] + notes[1:2]


def total_kernel(own, p1, p2, p3, first_ref, second_ref):
    def total(rows):
        return (own[rows, :].astype(F32) + p1[rows, :].astype(F32)) + (
            p2[rows, :].astype(F32) + p3[rows, :].astype(F32)
        )

    first_ref[0] = total(slice(0, D))
    second_ref[0, :, :HALF] = total(slice(D, D + UNITS))
    second_ref[0, :, HALF:] = total(slice(D + UNITS, PACKED))


def unpack_kernel(
    order_ref, home_ref, tok_ref, grad_ref, layer_ref, grad_out_ref, order_vmem, sem
):
    copy = pltpu.make_async_copy(order_ref, order_vmem, sem)
    copy.start()
    copy.wait()
    order = jnp.broadcast_to(order_vmem[...].astype(F32), (8, TOK)).astype(BF)
    token = iota((TOK, 2 * TOK), 0).astype(F32)
    token_pick, grad_pick = mixed_picks(TOK, True, slots=True)
    kind = (iota((TOK, 2 * TOK), 1) // BLK) % 2
    pick_token = ((token == dot(order, token_pick)[0:1]) & (kind == 0)).astype(BF)
    pick_grad = ((token == dot(order, grad_pick)[0:1]) & (kind == 1)).astype(BF)
    layer = tok_ref[...].astype(F32)
    grad = grad_ref[...].astype(F32)
    for half in range(ZH):
        rows = home_ref[half * 2 * TOK : (half + 1) * 2 * TOK, :]
        layer += dot(pick_token, rows)
        grad += dot(pick_grad, rows)
    layer_ref[...] = layer.astype(BF)
    grad_out_ref[...] = grad.astype(BF)


def in_hbm(value):
    return pltpu.with_memory_space_constraint(value, pltpu.HBM)


def call(kernel, outs, *operands, **options):
    return pl.pallas_call(
        kernel,
        out_shape=[
            out if hasattr(out, "memory_space") else jax.ShapeDtypeStruct(*out) for out in outs
        ],
        compiler_params=pltpu.CompilerParams(vmem_limit_bytes=VMEM_LIMIT),
        **options,
    )(*operands)


def shift(value, axis, size, by):
    return lax.ppermute(value, axis, [(i, (i + by) % size) for i in range(size)])


def on_device(tokens, slot_order, centroid, weight_in, weight_out, out_grad):
    vmem, hbm = pl.BlockSpec(memory_space=pltpu.VMEM), pl.BlockSpec(memory_space=pltpu.HBM)
    second = weight_out[0]
    shard = jnp.concatenate([weight_in[0], second[:, :HALF], second[:, HALF:]], axis=0)
    shards = [shard] + [shift(shard, "x", X, -k) for k in range(1, X)]
    token_scratch = [
        pltpu.VMEM((1, TOK), jnp.int32),
        pltpu.VMEM((TOK, D), BF),
        pltpu.VMEM((TOK, D), BF),
        pltpu.SemaphoreType.DMA((3,)),
    ]
    (packed,) = call(
        pack_kernel,
        [((MIXED, D), BF)],
        *(in_hbm(each) for each in (slot_order, tokens, out_grad)),
        in_specs=[hbm] * 3,
        out_specs=[vmem],
        scratch_shapes=token_scratch,
    )
    own_rows = lax.all_to_all(
        packed.reshape(ZH * EXPERTS, 2 * BLK, D), ("zh", "zl", "y"), 0, 0, tiled=True
    ).reshape(MIXED, D)
    other_rows = shift(own_rows, "core", CORE, 1)
    part_shapes = [
        ((MIXED, D), BF), ((1, D), F32), ((ROWS, D), BF), ((ROWS, D), BF),
        ((ROWS, X * UNITS), BF), ((ROWS, X * UNITS), BF),
    ]
    nothing = jnp.zeros((1, D), F32)
    other = call(expert_kernel, part_shapes, other_rows, centroid, nothing, *shards)
    own = call(expert_kernel, part_shapes, own_rows, centroid, other[1], *shards)
    from_other = shift(other[0], "core", CORE, 1)
    any_space = pl.BlockSpec(memory_space=pl.ANY)

    def weight_grads(shards, after):
        return call(
            functools.partial(weight_grad_kernel, shards),
            [((PACKED + 2 * NOTE, UNITS), BF)] * len(shards),
            *own[1:], *other[2:], after,
            in_specs=[vmem] * 9 + [any_space],
        )

    (returned,) = call(join_kernel, [((MIXED, D), BF)], own[0], from_other)
    p2, p1, p3, p0 = weight_grads((2, 1, 3, 0), from_other)
    arrived = [shift(p1, "x", X, 1), shift(p2, "x", X, 2), shift(p3, "x", X, 3)]
    home = lax.all_to_all(
        returned.reshape(ZH * EXPERTS, 2 * BLK, D), ("zh", "zl", "y"), 0, 0, tiled=True
    ).reshape(MIXED, D)
    (centroid_grad,) = call(note_kernel, [((1, D), F32)], own[1], *arrived)
    centroid_grad += shift(centroid_grad, "core", CORE, 1)
    grad_centroid = centroid_grad + shift(centroid_grad, "zh", ZH, 1)
    first_grad, second_grad = call(
        total_kernel,
        [((1, D, UNITS), F32), ((1, UNITS, D), F32)],
        p0, *arrived,
        cost_estimate=pl.CostEstimate(flops=20 * 10**9, transcendentals=0, bytes_accessed=4 * 2**20),
    )
    layer_out, grad_tokens = call(
        unpack_kernel,
        [((TOK, D), BF), ((TOK, D), BF)],
        in_hbm(slot_order), home, tokens, out_grad,
        in_specs=[hbm, vmem, vmem, vmem],
        scratch_shapes=[pltpu.VMEM((1, TOK), jnp.int32), pltpu.SemaphoreType.DMA(())],
    )
    return (layer_out, grad_tokens, grad_centroid, first_grad, second_grad)


def solution(mesh):
    fine = Mesh(mesh.devices.reshape(ZH, X, CORE, Y, ZL), ("zh", "x", "core", "y", "zl"))
    dp, expert = ("zh", "x", "core"), ("y", "zl")
    both = dp + expert
    placed = (
        P(both, None),
        P(both, None),
        P(expert, None),
        P(expert, None, dp),
        P(expert, dp, None),
        P(both, None),
    )
    return jax.shard_map(
        on_device,
        mesh=fine,
        in_specs=placed,
        out_specs=(
            P(both, None),
            P(both, None),
            P(expert, None),
            P(expert, None, dp),
            P(expert, dp, None),
        ),
        check_vma=False,
    )
```

```python
import functools
import math

import jax
import jax.numpy as jnp
from jax import lax
from jax.experimental import pallas as pl
from jax.experimental.pallas import tpu as pltpu
from jax.sharding import Mesh
from jax.sharding import PartitionSpec as P

BF = jnp.bfloat16
F32 = jnp.float32
ZH, X, CORE, Y, ZL = 2, 4, 2, 4, 8
EXPERTS = Y * ZL
BLK = 4
D = 512
TOK = EXPERTS * BLK
ROWS = ZH * TOK
MIXED = 2 * ROWS
UNITS = 256
HALF = D // 2
PACKED = D + 2 * UNITS
NOTE = 16
VMEM_LIMIT = 16 * 1024 * 1024


def dot(a, b, ca=1, cb=0):
    return lax.dot_general(a, b, (((ca,), (cb,)), ((), ())), preferred_element_type=F32)


def iota(shape, axis):
    return lax.broadcasted_iota(jnp.int32, shape, axis)


def mixed_picks(rows, on_rows_first, slots=False):
    shape = (rows, 2 * rows) if on_rows_first else (2 * rows, rows)
    plain = iota(shape, 0 if on_rows_first else 1)
    mixed = iota(shape, 1 if on_rows_first else 0)
    group = plain // BLK
    if slots:
        group = (group % ZL) * Y + group // ZL
    place = group * (2 * BLK) + plain % BLK
    return (mixed == place).astype(BF), (mixed == place + BLK).astype(BF)


def pack_kernel(
    order_ref, tok_ref, grad_ref, out_ref, order_vmem, tok_vmem, grad_vmem, sems
):
    copies = [
        pltpu.make_async_copy(source, target, sems.at[i])
        for i, (source, target) in enumerate(
            ((order_ref, order_vmem), (tok_ref, tok_vmem), (grad_ref, grad_vmem))
        )
    ]
    for copy in copies:
        copy.start()
    token_pick, grad_pick = mixed_picks(TOK, True, slots=True)
    source = iota((TOK, 2 * TOK), 0).astype(F32)
    kind = (iota((TOK, 2 * TOK), 1) // BLK) % 2
    copies[0].wait()
    order = jnp.broadcast_to(order_vmem[...].astype(F32), (8, TOK)).astype(BF)
    token_source = dot(order, token_pick)[0:1]
    grad_source = dot(order, grad_pick)[0:1]
    pick_token = ((source == token_source) & (kind == 0)).astype(BF)
    pick_grad = ((source == grad_source) & (kind == 1)).astype(BF)
    copies[1].wait()
    mixed = dot(pick_token, tok_vmem[...], 0, 0)
    copies[2].wait()
    mixed = (mixed + dot(pick_grad, grad_vmem[...], 0, 0)).astype(BF)
    for half in range(ZH):
        out_ref[half * 2 * TOK : (half + 1) * 2 * TOK, :] = mixed


def expert_kernel(
    rows_ref, centroid_ref, before_ref, s0, s1, s2, s3,
    mixed_ref, centroid_grad_ref, routed_ref, d_expert_ref, hidden_ref, d_hidden_ref,
):
    token_pick, grad_pick = mixed_picks(ROWS, True)
    received = rows_ref[...]
    routed = dot(token_pick, received)
    d_routed = dot(grad_pick, received)
    centroid = centroid_ref[...].astype(F32)
    gating = jax.nn.sigmoid(jnp.sum(routed * centroid, axis=1, keepdims=True))
    routed_half = routed.astype(BF)
    d_expert = (gating * d_routed).astype(BF)
    routed_ref[...] = routed_half
    d_expert_ref[...] = d_expert
    out_part = jnp.zeros((ROWS, D), F32)
    inner_part = jnp.zeros((ROWS, D), F32)
    scale = math.sqrt(2.0 / math.pi)
    d_expert_a, d_expert_b = d_expert[:, :HALF], d_expert[:, HALF:]
    for k, shard in enumerate((s0, s1, s2, s3)):
        w = shard[:D, :]
        v_a, v_b = shard[D : D + UNITS, :], shard[D + UNITS :, :]
        pre = dot(routed_half, w)
        square = pre * pre
        bend = jnp.tanh(scale * pre * (1.0 + 0.044715 * square))
        half_up = 0.5 * (1.0 + bend)
        hidden = (pre * half_up).astype(BF)
        slope = half_up + 0.5 * pre * (1.0 - bend * bend) * (
            scale * (1.0 + 3.0 * 0.044715 * square)
        )
        back = dot(d_expert_a, v_a, 1, 1) + dot(d_expert_b, v_b, 1, 1)
        d_hidden = (back * slope).astype(BF)
        out_part += jnp.concatenate([dot(hidden, v_a), dot(hidden, v_b)], axis=1)
        inner_part += dot(d_hidden, w, 1, 1)
        hidden_ref[:, k * UNITS : (k + 1) * UNITS] = hidden
        d_hidden_ref[:, k * UNITS : (k + 1) * UNITS] = d_hidden
    d_logit = jnp.sum(d_routed * out_part, axis=1, keepdims=True) * gating * (1.0 - gating)
    centroid_grad = before_ref[...] + jnp.sum(d_logit * routed, axis=0, keepdims=True)
    centroid_grad_ref[...] = centroid_grad
    layer_part = (gating * out_part).astype(BF)
    grad_part = (inner_part + d_logit * centroid).astype(BF)
    token_place, grad_place = mixed_picks(ROWS, False)
    mixed_ref[...] = (dot(token_place, layer_part) + dot(grad_place, grad_part)).astype(BF)


def join_kernel(own_ref, other_ref, out_ref):
    out_ref[...] = (own_ref[...].astype(F32) + other_ref[...].astype(F32)).astype(BF)


def weight_grad_kernel(
    shards, centroid_ref, routed_a, d_expert_a, hidden_a, d_hidden_a,
    routed_b, d_expert_b, hidden_b, d_hidden_b, after_ref, *packed_refs,
):
    high = centroid_ref[...].astype(BF).astype(F32)
    row = iota((NOTE, D), 0)
    note = jnp.where(row == 0, high, jnp.where(row == 1, centroid_ref[...] - high, 0.0)).astype(BF)
    for k, packed in zip(shards, packed_refs):
        units = slice(k * UNITS, (k + 1) * UNITS)
        first = dot(routed_a[...], d_hidden_a[:, units], 0, 0) + dot(
            routed_b[...], d_hidden_b[:, units], 0, 0
        )
        second = dot(hidden_a[:, units], d_expert_a[...], 0, 0) + dot(
            hidden_b[:, units], d_expert_b[...], 0, 0
        )
        packed[:D, :] = first.astype(BF)
        packed[D : D + UNITS, :] = second[:, :HALF].astype(BF)
        packed[D + UNITS : PACKED, :] = second[:, HALF:].astype(BF)
        packed[PACKED : PACKED + NOTE, :] = note[:, :HALF]
        packed[PACKED + NOTE :, :] = note[:, HALF:]


def note_kernel(own_centroid, p1, p2, p3, out_ref):
    for at, columns in ((PACKED, slice(0, HALF)), (PACKED + NOTE, slice(HALF, D))):
        rows = slice(at, at + NOTE)
        notes = p1[rows, :].astype(F32) + p2[rows, :].astype(F32) + p3[rows, :].astype(F32)
        out_ref[:, columns] = own_centroid[:, columns] + notes[0:1] + notes[1:2]


def total_kernel(
    own, p1, p2, p3, order_ref, first_ref, second_ref, pick_token_ref, pick_grad_ref, order_vmem, sem
):
    copy = pltpu.make_async_copy(order_ref, order_vmem, sem)
    copy.start()

    def total(rows):
        return (own[rows, :].astype(F32) + p1[rows, :].astype(F32)) + (
            p2[rows, :].astype(F32) + p3[rows, :].astype(F32)
        )

    first_ref[0] = total(slice(0, D))
    second_ref[0, :, :HALF] = total(slice(D, D + UNITS))
    second_ref[0, :, HALF:] = total(slice(D + UNITS, PACKED))
    copy.wait()
    order = jnp.broadcast_to(order_vmem[...].astype(F32), (8, TOK)).astype(BF)
    token = iota((TOK, 2 * TOK), 0).astype(F32)
    token_pick, grad_pick = mixed_picks(TOK, True, slots=True)
    kind = (iota((TOK, 2 * TOK), 1) // BLK) % 2
    pick_token_ref[...] = ((token == dot(order, token_pick)[0:1]) & (kind == 0)).astype(BF)
    pick_grad_ref[...] = ((token == dot(order, grad_pick)[0:1]) & (kind == 1)).astype(BF)


def unpack_kernel(
    pick_token, pick_grad, home_ref, tok_ref, grad_ref, here_ref, there_ref,
    layer_ref, grad_out_ref, centroid_grad_ref,
):
    layer = tok_ref[...].astype(F32)
    grad = grad_ref[...].astype(F32)
    for half in range(ZH):
        rows = home_ref[half * 2 * TOK : (half + 1) * 2 * TOK, :]
        layer += dot(pick_token[...], rows)
        grad += dot(pick_grad[...], rows)
    layer_ref[...] = layer.astype(BF)
    grad_out_ref[...] = grad.astype(BF)
    centroid_grad_ref[...] = here_ref[...] + there_ref[...]


def in_hbm(value):
    return pltpu.with_memory_space_constraint(value, pltpu.HBM)


def call(kernel, outs, *operands, **options):
    return pl.pallas_call(
        kernel,
        out_shape=[
            out if hasattr(out, "memory_space") else jax.ShapeDtypeStruct(*out) for out in outs
        ],
        compiler_params=pltpu.CompilerParams(vmem_limit_bytes=VMEM_LIMIT),
        **options,
    )(*operands)


def shift(value, axis, size, by):
    return lax.ppermute(value, axis, [(i, (i + by) % size) for i in range(size)])


def on_device(tokens, slot_order, centroid, weight_in, weight_out, out_grad):
    vmem, hbm = pl.BlockSpec(memory_space=pltpu.VMEM), pl.BlockSpec(memory_space=pltpu.HBM)
    second = weight_out[0]
    shard = jnp.concatenate([weight_in[0], second[:, :HALF], second[:, HALF:]], axis=0)
    shards = [shard] + [shift(shard, "x", X, -k) for k in range(1, X)]
    token_scratch = [
        pltpu.VMEM((1, TOK), jnp.int32),
        pltpu.VMEM((TOK, D), BF),
        pltpu.VMEM((TOK, D), BF),
        pltpu.SemaphoreType.DMA((3,)),
    ]
    (packed,) = call(
        pack_kernel,
        [((MIXED, D), BF)],
        *(in_hbm(each) for each in (slot_order, tokens, out_grad)),
        in_specs=[hbm] * 3,
        out_specs=[vmem],
        scratch_shapes=token_scratch,
    )
    own_rows = lax.all_to_all(
        packed.reshape(ZH * EXPERTS, 2 * BLK, D), ("zh", "zl", "y"), 0, 0, tiled=True
    ).reshape(MIXED, D)
    other_rows = shift(own_rows, "core", CORE, 1)
    part_shapes = [
        ((MIXED, D), BF), ((1, D), F32), ((ROWS, D), BF), ((ROWS, D), BF),
        ((ROWS, X * UNITS), BF), ((ROWS, X * UNITS), BF),
    ]
    nothing = jnp.zeros((1, D), F32)
    other = call(expert_kernel, part_shapes, other_rows, centroid, nothing, *shards)
    own = call(expert_kernel, part_shapes, own_rows, centroid, other[1], *shards)
    from_other = shift(other[0], "core", CORE, 1)
    any_space = pl.BlockSpec(memory_space=pl.ANY)

    def weight_grads(shards, after):
        return call(
            functools.partial(weight_grad_kernel, shards),
            [pltpu.VMEM((PACKED + 2 * NOTE, UNITS), BF)] * len(shards),
            *own[1:], *other[2:], after,
            in_specs=[vmem] * 9 + [any_space],
        )

    (returned,) = call(join_kernel, [((MIXED, D), BF)], own[0], from_other)
    p2, p1, p3, p0 = weight_grads((2, 1, 3, 0), from_other)
    arrived = [shift(p1, "x", X, 1), shift(p2, "x", X, 2), shift(p3, "x", X, 3)]
    home = lax.all_to_all(
        returned.reshape(ZH * EXPERTS, 2 * BLK, D), ("zh", "zl", "y"), 0, 0, tiled=True
    ).reshape(MIXED, D)
    (centroid_grad,) = call(note_kernel, [((1, D), F32)], own[1], *arrived)
    centroid_grad += shift(centroid_grad, "core", CORE, 1)
    first_grad, second_grad, *picks = call(
        total_kernel,
        [
            ((1, D, UNITS), F32), ((1, UNITS, D), F32), ((TOK, 2 * TOK), BF), ((TOK, 2 * TOK), BF),
        ],
        p0, *arrived, in_hbm(slot_order),
        in_specs=[vmem] * X + [hbm],
        scratch_shapes=[pltpu.VMEM((1, TOK), jnp.int32), pltpu.SemaphoreType.DMA(())],
        cost_estimate=pl.CostEstimate(flops=20 * 10**9, transcendentals=0, bytes_accessed=4 * 2**20),
    )
    layer_out, grad_tokens, grad_centroid = call(
        unpack_kernel,
        [((TOK, D), BF), ((TOK, D), BF), ((1, D), F32)],
        *picks, home, tokens, out_grad, centroid_grad, shift(centroid_grad, "zh", ZH, 1),
    )
    return (layer_out, grad_tokens, grad_centroid, first_grad, second_grad)


def solution(mesh):
    fine = Mesh(mesh.devices.reshape(ZH, X, CORE, Y, ZL), ("zh", "x", "core", "y", "zl"))
    dp, expert = ("zh", "x", "core"), ("y", "zl")
    both = dp + expert
    placed = (
        P(both, None),
        P(both, None),
        P(expert, None),
        P(expert, None, dp),
        P(expert, dp, None),
        P(both, None),
    )
    return jax.shard_map(
        on_device,
        mesh=fine,
        in_specs=placed,
        out_specs=(
            P(both, None),
            P(both, None),
            P(expert, None),
            P(expert, None, dp),
            P(expert, dp, None),
        ),
        check_vma=False,
    )
```

```python
import functools
import math

import jax
import jax.numpy as jnp
from jax import lax
from jax.experimental import pallas as pl
from jax.experimental.pallas import tpu as pltpu
from jax.sharding import Mesh
from jax.sharding import PartitionSpec as P

BF = jnp.bfloat16
F32 = jnp.float32
ZH, X, CORE, Y, ZL = 2, 4, 2, 4, 8
EXPERTS = Y * ZL
BLK = 4
D = 512
TOK = EXPERTS * BLK
ROWS = ZH * TOK
MIXED = 2 * ROWS
UNITS = 256
HALF = D // 2
PACKED = D + 2 * UNITS
NOTE = 16
VMEM_LIMIT = 16 * 1024 * 1024


def dot(a, b, ca=1, cb=0):
    return lax.dot_general(a, b, (((ca,), (cb,)), ((), ())), preferred_element_type=F32)


def iota(shape, axis):
    return lax.broadcasted_iota(jnp.int32, shape, axis)


def mixed_picks(rows, on_rows_first, slots=False):
    shape = (rows, 2 * rows) if on_rows_first else (2 * rows, rows)
    plain = iota(shape, 0 if on_rows_first else 1)
    mixed = iota(shape, 1 if on_rows_first else 0)
    group = plain // BLK
    if slots:
        group = (group % ZL) * Y + group // ZL
    place = group * (2 * BLK) + plain % BLK
    return (mixed == place).astype(BF), (mixed == place + BLK).astype(BF)


def pack_kernel(
    order_ref, tok_ref, grad_ref, out_ref, order_vmem, tok_vmem, grad_vmem, sems
):
    copies = [
        pltpu.make_async_copy(source, target, sems.at[i])
        for i, (source, target) in enumerate(
            ((order_ref, order_vmem), (tok_ref, tok_vmem), (grad_ref, grad_vmem))
        )
    ]
    for copy in copies:
        copy.start()
    token_pick, grad_pick = mixed_picks(TOK, True, slots=True)
    source = iota((TOK, 2 * TOK), 0).astype(F32)
    kind = (iota((TOK, 2 * TOK), 1) // BLK) % 2
    copies[0].wait()
    order = jnp.broadcast_to(order_vmem[...].astype(F32), (8, TOK)).astype(BF)
    token_source = dot(order, token_pick)[0:1]
    grad_source = dot(order, grad_pick)[0:1]
    pick_token = ((source == token_source) & (kind == 0)).astype(BF)
    pick_grad = ((source == grad_source) & (kind == 1)).astype(BF)
    copies[1].wait()
    mixed = dot(pick_token, tok_vmem[...], 0, 0)
    copies[2].wait()
    mixed = (mixed + dot(pick_grad, grad_vmem[...], 0, 0)).astype(BF)
    for half in range(ZH):
        out_ref[half * 2 * TOK : (half + 1) * 2 * TOK, :] = mixed


def expert_kernel(
    rows_ref, centroid_ref, before_ref, s0, s1, s2, s3,
    mixed_ref, centroid_grad_ref, routed_ref, d_expert_ref, hidden_ref, d_hidden_ref,
):
    token_pick, grad_pick = mixed_picks(ROWS, True)
    received = rows_ref[...]
    routed = dot(token_pick, received)
    d_routed = dot(grad_pick, received)
    centroid = centroid_ref[...].astype(F32)
    gating = jax.nn.sigmoid(jnp.sum(routed * centroid, axis=1, keepdims=True))
    routed_half = routed.astype(BF)
    d_expert = (gating * d_routed).astype(BF)
    routed_ref[...] = routed_half
    d_expert_ref[...] = d_expert
    out_part = jnp.zeros((ROWS, D), F32)
    inner_part = jnp.zeros((ROWS, D), F32)
    scale = math.sqrt(2.0 / math.pi)
    d_expert_a, d_expert_b = d_expert[:, :HALF], d_expert[:, HALF:]
    for k, shard in enumerate((s0, s1, s2, s3)):
        w = shard[:D, :]
        v_a, v_b = shard[D : D + UNITS, :], shard[D + UNITS :, :]
        pre = dot(routed_half, w)
        square = pre * pre
        bend = jnp.tanh(scale * pre * (1.0 + 0.044715 * square))
        half_up = 0.5 * (1.0 + bend)
        hidden = (pre * half_up).astype(BF)
        slope = half_up + 0.5 * pre * (1.0 - bend * bend) * (
            scale * (1.0 + 3.0 * 0.044715 * square)
        )
        back = dot(d_expert_a, v_a, 1, 1) + dot(d_expert_b, v_b, 1, 1)
        d_hidden = (back * slope).astype(BF)
        out_part += jnp.concatenate([dot(hidden, v_a), dot(hidden, v_b)], axis=1)
        inner_part += dot(d_hidden, w, 1, 1)
        hidden_ref[:, k * UNITS : (k + 1) * UNITS] = hidden
        d_hidden_ref[:, k * UNITS : (k + 1) * UNITS] = d_hidden
    d_logit = jnp.sum(d_routed * out_part, axis=1, keepdims=True) * gating * (1.0 - gating)
    centroid_grad = before_ref[...] + jnp.sum(d_logit * routed, axis=0, keepdims=True)
    centroid_grad_ref[...] = centroid_grad
    layer_part = (gating * out_part).astype(BF)
    grad_part = (inner_part + d_logit * centroid).astype(BF)
    token_place, grad_place = mixed_picks(ROWS, False)
    mixed_ref[...] = (dot(token_place, layer_part) + dot(grad_place, grad_part)).astype(BF)


def join_kernel(own_ref, other_ref, out_ref):
    out_ref[...] = (own_ref[...].astype(F32) + other_ref[...].astype(F32)).astype(BF)


def weight_grad_kernel(
    shards, centroid_ref, routed_a, d_expert_a, hidden_a, d_hidden_a,
    routed_b, d_expert_b, hidden_b, d_hidden_b, after_ref, *packed_refs,
):
    high = centroid_ref[...].astype(BF).astype(F32)
    row = iota((NOTE, D), 0)
    note = jnp.where(row == 0, high, jnp.where(row == 1, centroid_ref[...] - high, 0.0)).astype(BF)
    for k, packed in zip(shards, packed_refs):
        units = slice(k * UNITS, (k + 1) * UNITS)
        first = dot(routed_a[...], d_hidden_a[:, units], 0, 0) + dot(
            routed_b[...], d_hidden_b[:, units], 0, 0
        )
        second = dot(hidden_a[:, units], d_expert_a[...], 0, 0) + dot(
            hidden_b[:, units], d_expert_b[...], 0, 0
        )
        packed[:D, :] = first.astype(BF)
        packed[D : D + UNITS, :] = second[:, :HALF].astype(BF)
        packed[D + UNITS : PACKED, :] = second[:, HALF:].astype(BF)
        packed[PACKED : PACKED + NOTE, :] = note[:, :HALF]
        packed[PACKED + NOTE :, :] = note[:, HALF:]


def note_kernel(own_centroid, p1, p2, p3, out_ref):
    for at, columns in ((PACKED, slice(0, HALF)), (PACKED + NOTE, slice(HALF, D))):
        rows = slice(at, at + NOTE)
        notes = p1[rows, :].astype(F32) + p2[rows, :].astype(F32) + p3[rows, :].astype(F32)
        out_ref[:, columns] = own_centroid[:, columns] + notes[0:1] + notes[1:2]


def total_kernel(
    own, p1, p2, p3, order_ref, first_ref, second_ref, pick_token_ref, pick_grad_ref, order_vmem, sem
):
    copy = pltpu.make_async_copy(order_ref, order_vmem, sem)
    copy.start()

    def total(rows):
        return (own[rows, :].astype(F32) + p1[rows, :].astype(F32)) + (
            p2[rows, :].astype(F32) + p3[rows, :].astype(F32)
        )

    first_ref[0] = total(slice(0, D))
    second_ref[0, :, :HALF] = total(slice(D, D + UNITS))
    second_ref[0, :, HALF:] = total(slice(D + UNITS, PACKED))
    copy.wait()
    order = jnp.broadcast_to(order_vmem[...].astype(F32), (8, TOK)).astype(BF)
    token = iota((TOK, 2 * TOK), 0).astype(F32)
    token_pick, grad_pick = mixed_picks(TOK, True, slots=True)
    kind = (iota((TOK, 2 * TOK), 1) // BLK) % 2
    pick_token_ref[...] = ((token == dot(order, token_pick)[0:1]) & (kind == 0)).astype(BF)
    pick_grad_ref[...] = ((token == dot(order, grad_pick)[0:1]) & (kind == 1)).astype(BF)


def unpack_kernel(
    pick_token, pick_grad, home_ref, tok_ref, grad_ref, here_ref, there_ref,
    layer_ref, grad_out_ref, centroid_grad_ref,
):
    layer = tok_ref[...].astype(F32)
    grad = grad_ref[...].astype(F32)
    for half in range(ZH):
        rows = home_ref[half * 2 * TOK : (half + 1) * 2 * TOK, :]
        layer += dot(pick_token[...], rows)
        grad += dot(pick_grad[...], rows)
    layer_ref[...] = layer.astype(BF)
    grad_out_ref[...] = grad.astype(BF)
    centroid_grad_ref[...] = here_ref[...] + there_ref[...]


def in_hbm(value):
    return pltpu.with_memory_space_constraint(value, pltpu.HBM)


def call(kernel, outs, *operands, **options):
    return pl.pallas_call(
        kernel,
        out_shape=[
            out if hasattr(out, "memory_space") else jax.ShapeDtypeStruct(*out) for out in outs
        ],
        compiler_params=pltpu.CompilerParams(vmem_limit_bytes=VMEM_LIMIT),
        **options,
    )(*operands)


def shift(value, axis, size, by):
    return lax.ppermute(value, axis, [(i, (i + by) % size) for i in range(size)])


def on_device(tokens, slot_order, centroid, weight_in, weight_out, out_grad):
    vmem, hbm = pl.BlockSpec(memory_space=pltpu.VMEM), pl.BlockSpec(memory_space=pltpu.HBM)
    second = weight_out[0]
    shard = jnp.concatenate([weight_in[0], second[:, :HALF], second[:, HALF:]], axis=0)
    shards = [shard] + [shift(shard, "x", X, -k) for k in range(1, X)]
    token_scratch = [
        pltpu.VMEM((1, TOK), jnp.int32),
        pltpu.VMEM((TOK, D), BF),
        pltpu.VMEM((TOK, D), BF),
        pltpu.SemaphoreType.DMA((3,)),
    ]
    (packed,) = call(
        pack_kernel,
        [((MIXED, D), BF)],
        *(in_hbm(each) for each in (slot_order, tokens, out_grad)),
        in_specs=[hbm] * 3,
        out_specs=[vmem],
        scratch_shapes=token_scratch,
    )
    own_rows = lax.all_to_all(
        packed.reshape(ZH * EXPERTS, 2 * BLK, D), ("zh", "zl", "y"), 0, 0, tiled=True
    ).reshape(MIXED, D)
    other_rows = shift(own_rows, "core", CORE, 1)
    part_shapes = [
        ((MIXED, D), BF), ((1, D), F32), ((ROWS, D), BF), ((ROWS, D), BF),
        ((ROWS, X * UNITS), BF), ((ROWS, X * UNITS), BF),
    ]
    nothing = jnp.zeros((1, D), F32)
    other = call(expert_kernel, part_shapes, other_rows, centroid, nothing, *shards)
    own = call(expert_kernel, part_shapes, own_rows, centroid, other[1], *shards)
    from_other = shift(other[0], "core", CORE, 1)
    any_space = pl.BlockSpec(memory_space=pl.ANY)

    def weight_grads(shards, after):
        return call(
            functools.partial(weight_grad_kernel, shards),
            [pltpu.VMEM((PACKED + 2 * NOTE, UNITS), BF)] * len(shards),
            *own[1:], *other[2:], after,
            in_specs=[vmem] * 9 + [any_space],
        )

    (returned,) = call(join_kernel, [pltpu.VMEM((MIXED, D), BF)], own[0], from_other)
    p2, p1, p3, p0 = weight_grads((2, 1, 3, 0), from_other)
    arrived = [shift(p1, "x", X, 1), shift(p2, "x", X, 2), shift(p3, "x", X, 3)]
    home = lax.all_to_all(
        returned.reshape(ZH * EXPERTS, 2 * BLK, D), ("zh", "zl", "y"), 0, 0, tiled=True
    ).reshape(MIXED, D)
    (centroid_grad,) = call(note_kernel, [((1, D), F32)], own[1], *arrived)
    centroid_grad += shift(centroid_grad, "core", CORE, 1)
    first_grad, second_grad, *picks = call(
        total_kernel,
        [
            ((1, D, UNITS), F32), ((1, UNITS, D), F32), ((TOK, 2 * TOK), BF), ((TOK, 2 * TOK), BF),
        ],
        p0, *arrived, in_hbm(slot_order),
        in_specs=[vmem] * X + [hbm],
        scratch_shapes=[pltpu.VMEM((1, TOK), jnp.int32), pltpu.SemaphoreType.DMA(())],
        cost_estimate=pl.CostEstimate(flops=20 * 10**9, transcendentals=0, bytes_accessed=4 * 2**20),
    )
    layer_out, grad_tokens, grad_centroid = call(
        unpack_kernel,
        [((TOK, D), BF), ((TOK, D), BF), ((1, D), F32)],
        *picks, home, tokens, out_grad, centroid_grad, shift(centroid_grad, "zh", ZH, 1),
    )
    return (layer_out, grad_tokens, grad_centroid, first_grad, second_grad)


def solution(mesh):
    fine = Mesh(mesh.devices.reshape(ZH, X, CORE, Y, ZL), ("zh", "x", "core", "y", "zl"))
    dp, expert = ("zh", "x", "core"), ("y", "zl")
    both = dp + expert
    placed = (
        P(both, None),
        P(both, None),
        P(expert, None),
        P(expert, None, dp),
        P(expert, dp, None),
        P(both, None),
    )
    return jax.shard_map(
        on_device,
        mesh=fine,
        in_specs=placed,
        out_specs=(
            P(both, None),
            P(both, None),
            P(expert, None),
            P(expert, None, dp),
            P(expert, dp, None),
        ),
        check_vma=False,
    )
```
